256 devices in a mesh: ctx: 16 (over x, y_hi, core), dec: 8 (over z), tp: 2 (over y_lo).
Axes of the slice: x: 4, y: 4 (y_hi: 2, y_lo: 2; y = y_hi * 2 + y_lo), z: 8, core: 2. Of those that a mesh axis runs over, the one named last changes fastest.
Arguments:
- queries: bfloat16 [8, 4096, 8192], P('dec', 'ctx', 'tp'), may hold values from -6 to 6
- keys: bfloat16 [8, 4096, 512], P('dec', 'ctx', 'tp'), may hold values from -6 to 6
- values: bfloat16 [8, 4096, 512], P('dec', 'ctx', 'tp'), may hold values from -6 to 6
- dec_queries: bfloat16 [4, 128, 8192], P(None, 'dec', 'tp'), may hold values from -6 to 6
- dec_keys: bfloat16 [4, 128, 512], P(None, 'dec', 'tp'), may hold values from -6 to 6
- dec_values: bfloat16 [4, 128, 512], P(None, 'dec', 'tp'), may hold values from -6 to 6
- page_table: int32 [8, 32], replicated, may hold values from 0 to 7
- ctx_lengths: int32 [128], P('dec'), may hold values from 1 to 4096, as said below
Outputs:
- prefill_out: bfloat16 [8, 4096, 8192], P('dec', 'ctx', 'tp')
- decode_out: bfloat16 [4, 128, 8192], P(None, 'dec', 'tp')
The draws below stay inside these ranges and needn't reach their ends.
Inputs may be any that keep to these rules, and one draw needn't show every extreme that they name: Each decode group has a row with ctx_lengths equal to 4096.
All inputs are finite; a program needn't handle non-finite values.
Results may differ from the reference program's by a relative error of at most 0.02.
Values may be sent and summed in bfloat16 or wider, within the bound.
No kernel may reach another device: no remote copies, remote signals or barrier semaphores. Data moves between devices by JAX's collectives and lax.ppermute only.
A program may use at most 128 MiB of HBM per device.

```python
import math
import jax
import jax.numpy as jnp
from jax import lax

HQ = 64
KVH = 4
HD = 128
PAGE = 128
ROWS = 16
STEPS = 4
SEQ = 4096
SEQS = 8
PAGES = 32
DROWS = 128


def draw_queries(key, part):
    key = jax.random.fold_in(key, 1)
    result = jax.random.truncated_normal(key, -6.0, 6.0, (SEQS, SEQ, HQ * HD), jnp.float32)
    return result.astype(jnp.bfloat16)


def draw_keys(key, part):
    key = jax.random.fold_in(key, 2)
    result = jax.random.truncated_normal(key, -6.0, 6.0, (SEQS, SEQ, KVH * HD), jnp.float32)
    return result.astype(jnp.bfloat16)


def draw_dec_queries(key, part):
    key = jax.random.fold_in(key, 3)
    result = jax.random.truncated_normal(key, -6.0, 6.0, (STEPS, DROWS, HQ * HD), jnp.float32)
    return result.astype(jnp.bfloat16)


def draw_dec_keys(key, part):
    key = jax.random.fold_in(key, 4)
    result = jax.random.truncated_normal(key, -6.0, 6.0, (STEPS, DROWS, KVH * HD), jnp.float32)
    return result.astype(jnp.bfloat16)


def draw_ctx_lengths(key, part):
    key = jax.random.fold_in(key, 11)
    first, second = jax.random.split(key)
    lengths = jax.random.randint(first, (SEQS, ROWS), 1, SEQ + 1)
    chosen = jax.random.randint(second, (SEQS, 1), 0, ROWS)
    lengths = jnp.where(jnp.arange(ROWS)[None, :] == chosen, SEQ, lengths)
    return lengths.reshape(SEQS * ROWS).astype(jnp.int32)


def set_ends(entries, own_key, low, high):
    spot = [jax.random.randint(jax.random.fold_in(own_key, axis), (), 0, length) for axis, length in enumerate(entries.shape)]
    longest = entries.shape.index(max(entries.shape))
    beside = spot[:longest] + [(spot[longest] + 1) % entries.shape[longest]] + spot[longest + 1:]
    return entries.at[tuple(spot)].set(low).at[tuple(beside)].set(high)


def levels(rng, shape, shards, low, largest):
    def one(axis_at, parts):
        heights = jax.random.uniform(jax.random.fold_in(jax.random.fold_in(rng, 6), axis_at), (parts,), jnp.float32, low / len(shards), largest / len(shards))
        return jnp.repeat(jnp.exp(heights), shape[axis_at] // parts).reshape((-1,) + (1,) * (len(shape) - axis_at - 1))

    loudness = one(*shards[0])
    for cut in shards[1:]:
        loudness = loudness * one(*cut)
    return loudness


def centred(own_key, dims, deviation, bound, cuts=(), held_as=jnp.bfloat16):
    values = deviation * jax.random.normal(own_key, dims, jnp.float32)
    if cuts:
        values = values * levels(own_key, dims, cuts, -0.22, 0.18)
    return jnp.clip(values, -bound, bound).astype(held_as)


def setup_inputs(seed: int = 0) -> dict:
    arg_keys = jax.random.split(jax.random.key(seed), 9)
    queries = draw_queries(jax.random.fold_in(arg_keys[8], 71), 0)
    keys = draw_keys(jax.random.fold_in(arg_keys[8], 71), 0)
    values = centred(arg_keys[2], (SEQS, SEQ, KVH * HD), 1.0, 6.0, ((0, 8), (1, 16), (2, 2)))
    dec_queries = draw_dec_queries(jax.random.fold_in(arg_keys[8], 71), 0)
    dec_keys = draw_dec_keys(jax.random.fold_in(arg_keys[8], 71), 0)
    dec_values = centred(arg_keys[5], (STEPS, DROWS, KVH * HD), 1.0, 6.0, ((1, 8), (2, 2)))
    page_table = set_ends(jax.random.randint(arg_keys[6], (SEQS, PAGES), 0, SEQS), jax.random.fold_in(arg_keys[6], 1), 0, SEQS - 1).astype(jnp.int32)
    ctx_lengths = draw_ctx_lengths(jax.random.fold_in(arg_keys[8], 71), 0)
    return dict(queries=queries, keys=keys, values=values, dec_queries=dec_queries, dec_keys=dec_keys, dec_values=dec_values, page_table=page_table, ctx_lengths=ctx_lengths)


def prefill_one(queries_one, keys_one, values_one):
    seq = queries_one.shape[0]
    kv_heads = keys_one.shape[1] // HD
    group = queries_one.shape[1] // keys_one.shape[1]
    scale = HD ** -0.5
    shaped_q = queries_one.reshape(seq, kv_heads, group, HD)
    shaped_k = keys_one.reshape(seq, kv_heads, HD).astype(jnp.float32)
    shaped_v = values_one.reshape(seq, kv_heads, HD).astype(jnp.float32)
    block = math.gcd(seq, 256)
    key_pos = jnp.arange(seq, dtype=jnp.int32)

    def one_block(index):
        query_block = lax.dynamic_slice_in_dim(shaped_q, index * block, block, 0).astype(jnp.float32)
        query_pos = index * block + jnp.arange(block, dtype=jnp.int32)

        def one_head(head):
            scores = jnp.einsum("rgd,kd->grk", query_block[:, head], shaped_k[:, head]) * scale
            valid = key_pos[None, None, :] <= query_pos[None, :, None]
            scores = jnp.where(valid, scores, -jnp.inf)
            best = jnp.max(scores, axis=-1, keepdims=True)
            weights = jnp.where(valid, jnp.exp(scores - best), 0.0)
            total = jnp.sum(weights, axis=-1)
            summed = jnp.einsum("grk,kd->grd", weights.astype(jnp.bfloat16).astype(jnp.float32), shaped_v[:, head])
            return summed / total[:, :, None]

        result = lax.map(one_head, jnp.arange(kv_heads, dtype=jnp.int32))
        return jnp.transpose(result, (2, 0, 1, 3)).reshape(block, kv_heads * group * HD)

    result = lax.map(one_block, jnp.arange(seq // block, dtype=jnp.int32))
    return result.reshape(seq, -1).astype(jnp.bfloat16)


def decode_group(step_q, step_k, step_v, cache_k, cache_v, lengths):
    steps, rows = step_q.shape[0], step_q.shape[1]
    kv_heads = cache_k.shape[1] // HD
    group = step_q.shape[2] // cache_k.shape[1]
    seq = cache_k.shape[0]
    scale = HD ** -0.5
    shaped_q = step_q.reshape(steps, rows, kv_heads, group, HD).astype(jnp.float32)
    shaped_nk = step_k.reshape(steps, rows, kv_heads, HD).astype(jnp.float32)
    shaped_nv = step_v.reshape(steps, rows, kv_heads, HD).astype(jnp.float32)
    shaped_ck = cache_k.reshape(seq, kv_heads, HD).astype(jnp.float32)
    shaped_cv = cache_v.reshape(seq, kv_heads, HD).astype(jnp.float32)
    cache_valid = jnp.arange(seq, dtype=jnp.int32)[None, None, None, :] < lengths[None, :, None, None]
    new_valid = jnp.arange(steps)[None, :] <= jnp.arange(steps)[:, None]
    new_valid = new_valid[:, None, None, :]

    def one_head(head):
        query_h = shaped_q[:, :, head]
        cache_scores = jnp.einsum("srgd,ud->srgu", query_h, shaped_ck[:, head]) * scale
        cache_scores = jnp.where(cache_valid, cache_scores, -jnp.inf)
        new_scores = jnp.einsum("srgd,trd->srgt", query_h, shaped_nk[:, :, head]) * scale
        new_scores = jnp.where(new_valid, new_scores, -jnp.inf)
        best = jnp.maximum(jnp.max(cache_scores, axis=-1), jnp.max(new_scores, axis=-1))
        cache_w = jnp.where(cache_valid, jnp.exp(cache_scores - best[..., None]), 0.0)
        new_w = jnp.where(new_valid, jnp.exp(new_scores - best[..., None]), 0.0)
        total = jnp.sum(cache_w, axis=-1) + jnp.sum(new_w, axis=-1)
        summed = jnp.einsum("srgu,ud->srgd", cache_w.astype(jnp.bfloat16).astype(jnp.float32), shaped_cv[:, head])
        summed = summed + jnp.einsum("srgt,trd->srgd", new_w.astype(jnp.bfloat16).astype(jnp.float32), shaped_nv[:, :, head])
        return summed / total[..., None]

    result = lax.map(one_head, jnp.arange(kv_heads, dtype=jnp.int32))
    return jnp.transpose(result, (1, 2, 0, 3, 4)).reshape(steps, rows, -1)


def reference(queries, keys, values, dec_queries, dec_keys, dec_values, page_table, ctx_lengths):
    prefill_out = lax.map(lambda items: prefill_one(items[0], items[1], items[2]), (queries, keys, values))
    positions = jnp.arange(SEQ, dtype=jnp.int32)

    def one_group(index):
        source = page_table[index][positions // PAGE]
        cache_k = keys[source, positions]
        cache_v = values[source, positions]
        start = (index * ROWS).astype(jnp.int32)
        step_q = lax.dynamic_slice_in_dim(dec_queries, start, ROWS, 1)
        step_k = lax.dynamic_slice_in_dim(dec_keys, start, ROWS, 1)
        step_v = lax.dynamic_slice_in_dim(dec_values, start, ROWS, 1)
        lengths = lax.dynamic_slice_in_dim(ctx_lengths, start, ROWS, 0)
        return decode_group(step_q, step_k, step_v, cache_k, cache_v, lengths)

    decoded = lax.map(one_group, jnp.arange(SEQS, dtype=jnp.int32))
    decode_out = jnp.transpose(decoded, (1, 0, 2, 3)).reshape(STEPS, SEQS * ROWS, -1).astype(jnp.bfloat16)
    return (prefill_out, decode_out)
```

```python
import functools

import jax
import jax.numpy as jnp
from jax import lax
from jax.experimental import pallas as pl
from jax.experimental.pallas import tpu as pltpu
from jax.sharding import PartitionSpec as P

HD = 128
PAGE = 128
SCALE = HD**-0.5
LOG2E = 1.4426950408889634
CEXP = SCALE * LOG2E
SAFE = 50.0
NEG = -1e30
NT = (((1,), (1,)), ((), ()))
VMEM_LIMIT = 56 * 2**20
F32 = jnp.float32
BF16 = jnp.bfloat16


def dot_nt(a, b):
    return lax.dot_general(a, b, NT, preferred_element_type=F32)


def dot_nn(a, b):
    return jnp.dot(a, b, preferred_element_type=F32)


def prefill_kernel(
    meta, q_own, q_oth, own, rr, ll, yy, xa, xb, ry, ly, xya, xyb, o_own, o_oth,
    ks, vx, acc, mx, sem, *, group, rows, first_head,
):
    chip, core, xpos, ypos = meta[0], meta[1], meta[2], meta[3]
    step = pl.program_id(0)
    half = 256

    def chip_id(dx, dy):
        return lax.rem(xpos + dx + 4, 4) * 2 + lax.rem(ypos + dy, 2)

    pieces = [
        (chip_id(0, 0), own, 0, own, 512),
        (chip_id(-1, 0), rr, 0, rr, 512),
        (chip_id(1, 0), ll, 0, ll, 512),
        (chip_id(0, 1), yy, 0, yy, 512),
        (chip_id(2, 0), xa, 0, xb, 0),
        (chip_id(-1, 1), ry, 0, ry, 512),
        (chip_id(1, 1), ly, 0, ly, 512),
        (chip_id(2, 1), xya, 0, xyb, 0),
    ]

    def copies(index):
        where, buf_a, off_a, buf_b, off_b = pieces[index]
        base = where * 512
        out = []
        for slot, (buf, off, place) in enumerate(((buf_a, off_a, 0), (buf_b, off_b, half))):
            dst = pl.multiple_of(base + place, half)
            out.append(
                pltpu.make_async_copy(
                    buf.at[pl.ds(off, half), :], ks.at[pl.ds(dst, half), :], sem.at[index, 2 * slot]
                )
            )
            out.append(
                pltpu.make_async_copy(
                    buf.at[pl.ds(off + half, half), :],
                    vx.at[pl.ds(dst, half), pl.ds(0, HD)],
                    sem.at[index, 2 * slot + 1],
                )
            )
        return out

    @pl.when(step == 0)
    def _load():
        for index in range(8):

            @pl.when(pieces[index][0] <= chip)
            def _start(index=index):
                for copy in copies(index):
                    copy.start()

        vx[:, HD:] = jnp.ones((vx.shape[0], HD), BF16)
        for index in range(8):

            @pl.when(pieces[index][0] <= chip)
            def _wait(index=index):
                for copy in copies(index):
                    copy.wait()

        def norm(block, best):
            rows_k = ks[pl.ds(pl.multiple_of(block * 512, 512), 512), :].astype(F32)
            sums = jnp.sum(rows_k * rows_k, axis=1, keepdims=True)
            return jnp.maximum(best, jnp.max(sums, axis=0, keepdims=True))

        mx[0, 0:1, 0:1] = lax.fori_loop(0, chip + 1, norm, jnp.zeros((1, 1), F32))

    kmax = mx[0, 0:1, 0:1]
    q_refs = (q_own, q_oth)

    qmax = jnp.zeros((1, 1), F32)
    for q_ref in q_refs:
        for g in range(group):
            block = q_ref[:, g * HD : (g + 1) * HD].astype(F32)
            sums = jnp.sum(block * block, axis=1, keepdims=True)
            qmax = jnp.maximum(qmax, jnp.max(sums, axis=0, keepdims=True))
    bound = qmax * kmax * (SCALE * SCALE * 1.0001)
    safe = bound[0, 0] <= SAFE * SAFE
    own_base = pl.multiple_of(chip * 512, 512)

    @pl.when(safe)
    def _plain():
        for side in range(2):
            keys = ks[pl.ds(pl.multiple_of(own_base + side * half, half), half), :]
            vals = vx[pl.ds(pl.multiple_of(own_base + side * half, half), half), :]
            for g in range(group):
                for r in range(half // rows):
                    rs = slice(r * rows, (r + 1) * rows)
                    s = dot_nt(q_refs[side][rs, g * HD : (g + 1) * HD], keys) * CEXP
                    ok = lax.broadcasted_iota(jnp.int32, s.shape, 1) <= (
                        lax.broadcasted_iota(jnp.int32, s.shape, 0) + r * rows
                    )
                    p = jnp.where(ok, jnp.exp2(s), 0.0).astype(BF16)
                    acc[g, side * half + r * rows : side * half + (r + 1) * rows, :] = dot_nn(p, vals)

        def block_of(base, size, sides):
            keys = ks[pl.ds(base, size), :]
            vals = vx[pl.ds(base, size), :]
            for g in range(group):
                for side in sides:
                    for r in range(half // rows):
                        rs = slice(r * rows, (r + 1) * rows)
                        at = slice(side * half + r * rows, side * half + (r + 1) * rows)
                        s = dot_nt(q_refs[side][rs, g * HD : (g + 1) * HD], keys) * CEXP
                        p = jnp.exp2(s).astype(BF16)
                        acc[g, at, :] += dot_nn(p, vals)

        @pl.when(core == 0)
        def _late_other():
            block_of(pl.multiple_of(own_base, half), half, (1,))

        @pl.when(core == 1)
        def _late_own():
            block_of(pl.multiple_of(own_base + half, half), half, (0,))

        def pair(index, carry):
            block_of(pl.multiple_of(index * 1024, 1024), 1024, (0, 1))
            return carry

        lax.fori_loop(0, chip // 2, pair, 0)

        @pl.when(lax.rem(chip, 2) == 1)
        def _last():
            block_of(pl.multiple_of((chip - 1) * 512, 512), 512, (0, 1))

    @pl.when(jnp.logical_not(safe))
    def _online():
        for side in range(2):
            q_pos0 = jnp.where(side == 0, core, 1 - core) * half
            for g in range(group):
                at = slice(side * half, (side + 1) * half)
                q_block = q_refs[side][:, g * HD : (g + 1) * HD]
                acc[g, at, :] = jnp.zeros((half, 2 * HD), F32)

                def one(index, best, q_block=q_block, g=g, at=at, q_pos0=q_pos0):
                    base = pl.multiple_of(index * half, half)
                    s = dot_nt(q_block, ks[pl.ds(base, half), :]) * SCALE
                    place = lax.rem(index, 2)
                    k_pos0 = jnp.where(place == 0, core, 1 - core) * half
                    shift = jnp.where(index < 2 * chip, 4 * half, q_pos0 - k_pos0)
                    ok = lax.broadcasted_iota(jnp.int32, s.shape, 1) <= (
                        lax.broadcasted_iota(jnp.int32, s.shape, 0) + shift
                    )
                    s = jnp.where(ok, s, NEG)
                    new = jnp.maximum(best, jnp.max(s, axis=1, keepdims=True))
                    p = jnp.where(ok, jnp.exp(s - new), 0.0).astype(BF16)
                    acc[g, at, :] = acc[g, at, :] * jnp.exp(best - new) + dot_nn(
                        p, vx[pl.ds(base, half), :]
                    )
                    return new

                lax.fori_loop(0, 2 * chip + 2, one, jnp.full((half, 1), NEG, F32))

    for g in range(group):
        for side, o_ref in enumerate((o_own, o_oth)):
            at = slice(side * half, (side + 1) * half)
            o_ref[:, g * HD : (g + 1) * HD] = (acc[g, at, :HD] / acc[g, at, HD:]).astype(BF16)


def prefill(meta, queries, q_oth, bufs, first_head, heads, group=4, rows=128):
    per = 16 // group
    first = first_head // group
    any_spec = pl.BlockSpec(memory_space=pl.ANY)
    flops = 4 * 512 * heads * 2048 * HD * 2
    return pl.pallas_call(
        functools.partial(prefill_kernel, group=group, rows=rows, first_head=first_head),
        grid_spec=pltpu.PrefetchScalarGridSpec(
            num_scalar_prefetch=1,
            grid=(heads // group,),
            in_specs=[
                pl.BlockSpec((256, group * HD), lambda i, m: (0, m[1] * per + first + i)),
                pl.BlockSpec((256, group * HD), lambda i, m: (0, first + i)),
            ]
            + [any_spec] * 10,
            out_specs=[pl.BlockSpec((256, group * HD), lambda i, m: (0, i))] * 2,
            scratch_shapes=[
                pltpu.VMEM((4096, HD), BF16),
                pltpu.VMEM((4096, 2 * HD), BF16),
                pltpu.VMEM((group, 512, 2 * HD), F32),
                pltpu.VMEM((1, 8, 128), F32),
                pltpu.SemaphoreType.DMA((8, 4)),
            ],
        ),
        out_shape=[jax.ShapeDtypeStruct((256, heads * HD), BF16)] * 2,
        compiler_params=pltpu.CompilerParams(vmem_limit_bytes=VMEM_LIMIT),
        cost_estimate=pl.CostEstimate(flops=flops, bytes_accessed=8 * 2**20, transcendentals=0),
        name="prefill",
    )(meta, queries, q_oth, *bufs)


def decode_kernel(
    meta, table, q_ref, nk_ref, nv_ref, len_ref, own, f1, f2, f3, b1, b2, b3, f4, b4,
    keep, send, ks, vx, sem,
):
    chip, core, zpos, mask = meta[0], meta[1], meta[4], meta[5]
    sources = {0: own, 7: f1, 6: f2, 5: f3, 1: b1, 2: b2, 3: b3}

    def page_copy(buf, off, page):
        return (
            pltpu.make_async_copy(
                buf.at[pl.ds(off, PAGE), :], ks.at[pl.ds(page * PAGE, PAGE), :], sem.at[page, 0]
            ),
            pltpu.make_async_copy(
                buf.at[pl.ds(off + 256, PAGE), :],
                vx.at[pl.ds(page * PAGE, PAGE), pl.ds(0, HD)],
                sem.at[page, 1],
            ),
        )

    for page in range(4):
        side, inner = page // 2, page % 2
        from_core = core if side == 0 else 1 - core
        prompt = table[zpos, chip * 4 + from_core * 2 + inner]
        rel = lax.rem(prompt - zpos + 8, 8)
        for r in range(8):
            if r == 4:
                buf, off = (f4, b4)[side], inner * PAGE
            else:
                buf, off = sources[r], side * 512 + inner * PAGE

            @pl.when(rel == r)
            def _start(buf=buf, off=off, page=page):
                for copy in page_copy(buf, off, page):
                    copy.start()

    vx[:, HD:] = jnp.ones((512 + 64, HD), BF16)
    ks[512:, :] = nk_ref[...].reshape(64, HD)
    vx[512:, :HD] = nv_ref[...].reshape(64, HD)
    for page in range(4):
        for copy in page_copy(own, 0, page):
            copy.wait()

    lens = len_ref[...]
    row = lax.broadcasted_iota(jnp.int32, (64, 64), 0)
    col = lax.broadcasted_iota(jnp.int32, (64, 64), 1)
    new_ok = (lax.rem(row, 16) == lax.rem(col, 16)) & (col <= row) & (chip == 0)
    pos = lax.broadcasted_iota(jnp.int32, (64, 256), 1)
    base = chip * 512
    ok0 = pos + (base + core * 256) < lens
    ok1 = pos + (base + (1 - core) * 256) < lens
    ok = jnp.concatenate([ok0, ok1, new_ok], axis=1)
    keys = ks[...]
    vals = vx[...]
    lane = lax.broadcasted_iota(jnp.int32, (64, HD), 1)
    for part, out in enumerate((keep, send)):
        stats = jnp.zeros((64, HD), F32)
        for g in range(8):
            head = (part * 8 + g) ^ mask
            q = q_ref[:, :, pl.ds(pl.multiple_of(head * HD, HD), HD)].reshape(64, HD)
            s = jnp.where(ok, dot_nt(q, keys) * SCALE, NEG)
            best = jnp.max(s, axis=1, keepdims=True).astype(BF16).astype(F32)
            p = jnp.where(ok, jnp.exp(s - best), 0.0).astype(BF16)
            o = dot_nn(p, vals)
            out[:, g * HD : (g + 1) * HD] = o[:, :HD].astype(BF16)
            total = o[:, HD : HD + 1]
            high = total.astype(BF16).astype(F32)
            stats = jnp.where(lane == g, best, stats)
            stats = jnp.where(lane == 16 + g, high, stats)
            stats = jnp.where(lane == 32 + g, total - high, stats)
        out[:, 8 * HD :] = stats.astype(BF16)


def decode_part(meta, table, dec_q, dec_k, dec_v, lens, bufs):
    any_spec = pl.BlockSpec(memory_space=pl.ANY)
    shape = jax.ShapeDtypeStruct((64, 9 * HD), BF16)
    return pl.pallas_call(
        decode_kernel,
        grid_spec=pltpu.PrefetchScalarGridSpec(
            num_scalar_prefetch=2,
            grid=(1,),
            in_specs=[
                pl.BlockSpec((4, 16, 16 * HD), lambda i, m, t: (0, 0, m[1])),
                pl.BlockSpec((4, 16, HD), lambda i, m, t: (0, 0, m[1])),
                pl.BlockSpec((4, 16, HD), lambda i, m, t: (0, 0, m[1])),
                pl.BlockSpec((64, 1), lambda i, m, t: (0, 0)),
            ]
            + [any_spec] * 9,
            out_specs=[pl.BlockSpec((64, 9 * HD), lambda i, m, t: (0, 0))] * 2,
            scratch_shapes=[
                pltpu.VMEM((512 + 64, HD), BF16),
                pltpu.VMEM((512 + 64, 2 * HD), BF16),
                pltpu.SemaphoreType.DMA((4, 2)),
            ],
        ),
        out_shape=[shape, shape],
        compiler_params=pltpu.CompilerParams(vmem_limit_bytes=VMEM_LIMIT),
        cost_estimate=pl.CostEstimate(flops=2 * 10**9, bytes_accessed=2**20, transcendentals=0),
        name="decode_part",
    )(meta, table, dec_q, dec_k, dec_v, lens, *bufs)


def merge_kernel(a_ref, b_ref, *outs, heads):
    lane = lax.broadcasted_iota(jnp.int32, (64, HD), 1)
    stat_a = a_ref[:, heads * HD :].astype(F32)
    stat_b = b_ref[:, heads * HD :].astype(F32)
    last = len(outs) == 1
    each = heads if last else heads // 2
    for part, out in enumerate(outs):
        stats = jnp.zeros((64, HD), F32)
        for g in range(each):
            h = part * each + g
            m_a, m_b = stat_a[:, h : h + 1], stat_b[:, h : h + 1]
            l_a = stat_a[:, 16 + h : 17 + h] + stat_a[:, 32 + h : 33 + h]
            l_b = stat_b[:, 16 + h : 17 + h] + stat_b[:, 32 + h : 33 + h]
            best = jnp.maximum(m_a, m_b)
            w_a, w_b = jnp.exp(m_a - best), jnp.exp(m_b - best)
            cols = slice(h * HD, (h + 1) * HD)
            total = l_a * w_a + l_b * w_b
            summed = a_ref[:, cols].astype(F32) * w_a + b_ref[:, cols].astype(F32) * w_b
            if last:
                out[:, g * HD : (g + 1) * HD] = (summed / total).astype(BF16)
            else:
                out[:, g * HD : (g + 1) * HD] = summed.astype(BF16)
                high = total.astype(BF16).astype(F32)
                stats = jnp.where(lane == g, best, stats)
                stats = jnp.where(lane == 16 + g, high, stats)
                stats = jnp.where(lane == 32 + g, total - high, stats)
        if not last:
            out[:, each * HD :] = stats.astype(BF16)


def merge(a, b, heads, last=False):
    if last:
        shapes = [jax.ShapeDtypeStruct((64, heads * HD), BF16)]
    else:
        shapes = [jax.ShapeDtypeStruct((64, (heads // 2 + 1) * HD), BF16)] * 2
    out = pl.pallas_call(
        functools.partial(merge_kernel, heads=heads),
        out_shape=shapes,
        cost_estimate=pl.CostEstimate(flops=10**6, bytes_accessed=2**18, transcendentals=0),
        name="merge",
    )(a, b)
    return out[0] if last else out


def place_kernel(meta, own, oth, out):
    core, mask = meta[1], meta[5]
    for side, ref in enumerate((own, oth)):
        which = core if side == 0 else 1 - core
        for b in range(8):
            at = which * 16 + ((2 * b) ^ mask)
            out[:, :, pl.ds(pl.multiple_of(at * HD, 2 * HD), 2 * HD)] = ref[
                :, b * 2 * HD : (b + 1) * 2 * HD
            ].reshape(4, 16, 2 * HD)


def place(meta, own, oth):
    return pl.pallas_call(
        place_kernel,
        grid_spec=pltpu.PrefetchScalarGridSpec(
            num_scalar_prefetch=1,
            grid=(1,),
            in_specs=[pl.BlockSpec((64, 2048), lambda i, m: (0, 0))] * 2,
            out_specs=pl.BlockSpec((4, 16, 4096), lambda i, m: (0, 0, 0)),
        ),
        out_shape=jax.ShapeDtypeStruct((4, 16, 4096), BF16),
        name="place",
    )(meta, own, oth)


def ctx_move(array, dx=0, flip_y=0, flip_core=0, mirror_x=0):
    pairs = []
    for c in range(16):
        x, y, core = c // 4, (c // 2) % 2, c % 2
        to_x = ((x + dx) % 4) ^ mirror_x
        pairs.append((c, to_x * 4 + (y ^ flip_y) * 2 + (core ^ flip_core)))
    return lax.ppermute(array, "ctx", pairs)


def dec_move(array, dz):
    return lax.ppermute(array, "dec", [(i, (i + dz) % 8) for i in range(8)])


def body(queries, keys, values, dec_queries, dec_keys, dec_values, page_table, ctx_lengths):
    c = lax.axis_index("ctx")
    z = lax.axis_index("dec")
    x, y, core = c // 4, (c // 2) % 2, c % 2
    chip = c // 2
    mask = y * 8 + ((x ^ (x >> 1)) & 1) * 4 + (x >> 1) * 2
    meta = jnp.stack([chip, core, x, y, z, mask]).astype(jnp.int32)

    k0, v0 = keys[0], values[0]
    first = jnp.concatenate([k0[:, :HD], v0[:, :HD]], axis=0)
    second = jnp.concatenate([k0[:, HD:], v0[:, HD:]], axis=0)
    mine = jnp.where(core == 0, first, second)
    other = jnp.where(core == 0, second, first)
    chunk = jnp.concatenate([mine, ctx_move(other, flip_core=1)], axis=0)
    q_send = lax.dynamic_slice_in_dim(queries[0], (1 - core) * 2048, 2048, 1)

    f1, b1 = dec_move(chunk, 1), dec_move(chunk, -1)
    rr, ll, yy = ctx_move(chunk, dx=1), ctx_move(chunk, dx=-1), ctx_move(chunk, flip_y=1)
    q_oth = ctx_move(q_send, flip_core=1)
    f2, b2 = dec_move(f1, 1), dec_move(b1, -1)
    xa, xb = ctx_move(rr[:512], dx=1), ctx_move(ll[512:], dx=-1)
    ry, ly = ctx_move(yy, dx=1), ctx_move(yy, dx=-1)
    f3, b3 = dec_move(f2, 1), dec_move(b2, -1)
    xya, xyb = ctx_move(ry[:512], dx=1), ctx_move(ly[512:], dx=-1)
    f4, b4 = dec_move(f3[:512], 1), dec_move(b3[512:], -1)

    bufs = (chunk, rr, ll, yy, xa, xb, ry, ly, xya, xyb)
    pieces = 2
    outs = []
    for piece in range(pieces):
        o_own, o_send = prefill(meta, queries[0], q_oth, bufs, piece * 16 // pieces, 16 // pieces)
        outs.append((o_own, ctx_move(o_send, flip_core=1)))
    own_out = jnp.concatenate([o[0] for o in outs], axis=1)
    oth_out = jnp.concatenate([o[1] for o in outs], axis=1)
    prefill_out = jnp.where(
        core == 0,
        jnp.concatenate([own_out, oth_out], axis=1),
        jnp.concatenate([oth_out, own_out], axis=1),
    )[None]

    lens = jnp.tile(ctx_lengths, 4)[:, None]
    keep, send = decode_part(
        meta, page_table, dec_queries, dec_keys, dec_values, lens, (chunk, f1, f2, f3, b1, b2, b3, f4, b4)
    )
    keep, send = merge(keep, ctx_move(send, flip_y=1), 8)
    keep, send = merge(keep, ctx_move(send, mirror_x=1), 4)
    part = merge(keep, ctx_move(send, mirror_x=3), 2, last=True)
    part = jnp.concatenate([part, ctx_move(part, mirror_x=3)], axis=1)
    part = jnp.concatenate([part, ctx_move(part, mirror_x=1)], axis=1)
    part = jnp.concatenate([part, ctx_move(part, flip_y=1)], axis=1)
    decode_out = place(meta, part, ctx_move(part, flip_core=1))
    return (prefill_out, decode_out)


def solution(mesh):
    return jax.shard_map(
        body,
        mesh=mesh,
        in_specs=(
            P("dec", "ctx", "tp"),
            P("dec", "ctx", "tp"),
            P("dec", "ctx", "tp"),
            P(None, "dec", "tp"),
            P(None, "dec", "tp"),
            P(None, "dec", "tp"),
            P(),
            P("dec"),
        ),
        out_specs=(P("dec", "ctx", "tp"), P(None, "dec", "tp")),
        check_vma=False,
    )
```

```python
import functools

import jax
import jax.numpy as jnp
from jax import lax
from jax.experimental import pallas as pl
from jax.experimental.pallas import tpu as pltpu
from jax.sharding import PartitionSpec as P

HD = 128
PAGE = 128
SCALE = HD**-0.5
LOG2E = 1.4426950408889634
CEXP = SCALE * LOG2E
SAFE = 75.0
NEG = -1e30
NT = (((1,), (1,)), ((), ()))
VMEM_LIMIT = 56 * 2**20
SMALL_LIMIT = 16 * 2**20
F32 = jnp.float32
BF16 = jnp.bfloat16


def dot_nt(a, b):
    return lax.dot_general(a, b, NT, preferred_element_type=F32)


def dot_nn(a, b):
    return jnp.dot(a, b, preferred_element_type=F32)


def row_norm_bound(block, fold):
    sq = block.astype(F32)
    sq = sq * sq
    each = sq.shape[0] // fold
    most = sq[:each]
    for i in range(1, fold):
        most = jnp.maximum(most, sq[i * each : (i + 1) * each])
    return jnp.max(jnp.sum(most, axis=1, keepdims=True), axis=0, keepdims=True)


def prefill_kernel(meta, *refs, group, rows, first):
    chip, core, xpos, ypos = meta[0], meta[1], meta[2], meta[3]
    if first:
        q_own, q_oth, own, rr, ll, yy, state, flag, ks, vx, kbest, sem = refs
    else:
        q_own, q_oth, ry, ly, xx, xy, before_a, flag_a, before_b, flag_b = refs[:10]
        o_own, o_oth, ks, vx, kbest, acc, sem = refs[-7:]
    step = pl.program_id(0)
    half = 256

    def chip_id(dx, dy):
        return lax.rem(xpos + dx + 4, 4) * 2 + lax.rem(ypos + dy, 2)

    if first:
        pieces = [(chip_id(0, 0), own), (chip_id(-1, 0), rr), (chip_id(1, 0), ll), (chip_id(0, 1), yy)]
    else:
        pieces = [(chip_id(-1, 1), ry), (chip_id(1, 1), ly), (chip_id(2, 0), xx), (chip_id(2, 1), xy)]
    needed = [p[0] <= chip for p in pieces]
    slots, count = [], jnp.int32(0)
    for need in needed:
        slots.append(count)
        count = count + need.astype(jnp.int32)

    def copies(index):
        buf = pieces[index][1]
        base = slots[index] * 512
        out = []
        for side in range(2):
            off = side * 512
            dst = pl.multiple_of(base + side * half, half)
            out.append(
                pltpu.make_async_copy(
                    buf.at[pl.ds(off, half), :], ks.at[pl.ds(dst, half), :], sem.at[index, 2 * side]
                )
            )
            out.append(
                pltpu.make_async_copy(
                    buf.at[pl.ds(off + half, half), :],
                    vx.at[pl.ds(dst, half), pl.ds(0, HD)],
                    sem.at[index, 2 * side + 1],
                )
            )
        return out

    @pl.when(step == 0)
    def _load():
        for index in range(4):

            @pl.when(needed[index])
            def _start(index=index):
                for copy in copies(index):
                    copy.start()

        vx[:, HD:] = jnp.ones((vx.shape[0], HD), BF16)
        for index in range(4):

            @pl.when(needed[index])
            def _wait(index=index):
                for copy in copies(index):
                    copy.wait()

        def norm(block, best):
            return jnp.maximum(best, row_norm_bound(ks[pl.ds(pl.multiple_of(block * 512, 512), 512), :], 8))

        kbest[0:1, 0:1] = lax.fori_loop(0, count, norm, jnp.zeros((1, 1), F32))

    q_refs = (q_own, q_oth)
    qmax = jnp.zeros((1, 1), F32)
    for q_ref in q_refs:
        for g in range(group):
            qmax = jnp.maximum(qmax, row_norm_bound(q_ref[:, g * HD : (g + 1) * HD], 4))
    bound = qmax * kbest[0:1, 0:1] * (SCALE * SCALE * 1.0001)
    safe = bound[0, 0] <= SAFE * SAFE
    if first:
        flag[step] = jnp.where(safe, 0, 1)
    else:
        later = step >= flag_a.shape[0]
        shifted = jnp.where(later, flag_b[lax.rem(step, flag_b.shape[0])], flag_a[lax.rem(step, flag_a.shape[0])]) != 0
        safe = safe & jnp.logical_not(shifted)

    def tiles():
        for g in range(group):
            for side in range(2):
                for r in range(half // rows):
                    q = q_refs[side][r * rows : (r + 1) * rows, g * HD : (g + 1) * HD]
                    yield g, side, r, slice(side * half + r * rows, side * half + (r + 1) * rows), q

    def allowed(side, r):
        q_pos0 = (core if side == 0 else 1 - core) * half + r * rows
        row = lax.broadcasted_iota(jnp.int32, (rows, half), 0) + q_pos0
        col = lax.broadcasted_iota(jnp.int32, (rows, half), 1)
        return jnp.concatenate([col + core * half <= row, col + (1 - core) * half <= row], axis=1)

    def weighted(q, base, size, ok=None):
        p = jnp.exp2(dot_nt(q, ks[pl.ds(base, size), :]) * CEXP)
        if ok is not None:
            masked = jnp.where(ok, p[:, :512], 0.0)
            p = masked if size == 512 else jnp.concatenate([masked, p[:, 512:]], axis=1)
        return dot_nn(p.astype(BF16), vx[pl.ds(base, size), :])

    def write(g, side, at, both):
        cols = slice(g * HD, (g + 1) * HD)
        r = slice(at.start - side * half, at.stop - side * half)
        (o_own, o_oth)[side][r, cols] = (both[:, :HD] / both[:, HD:]).astype(BF16)

    full = count == 4

    def started(g, at):
        return jnp.where(later, before_b[g, at, :], before_a[g, at, :])


    @pl.when(safe & full)
    def _straight():
        for g, side, r, at, q in tiles():
            if first:
                state[g, at, :] = weighted(q, 0, 2048, allowed(side, r))
            else:
                write(g, side, at, started(g, at) + weighted(q, 0, 2048))

    @pl.when(safe & jnp.logical_not(full))
    def _plain():
        sums = state if first else acc
        for g, side, r, at, q in tiles():
            if first:
                sums[g, at, :] = weighted(q, 0, 512, allowed(side, r))
            else:
                sums[g, at, :] = started(g, at)

        def one(index, carry):
            for g, side, r, at, q in tiles():
                sums[g, at, :] += weighted(q, pl.multiple_of(index * 512, 512), 512)
            return carry

        lax.fori_loop(1 if first else 0, count, one, 0)
        if not first:
            for g, side, r, at, q in tiles():
                write(g, side, at, sums[g, at, :])

    @pl.when(jnp.logical_not(safe))
    def _online():
        sums = state if first else acc
        lane = lax.broadcasted_iota(jnp.int32, (rows, 2 * HD), 1)
        for g, side, r, at, q in tiles():
            if first:
                sums[g, at, :] = jnp.zeros((rows, 2 * HD), F32)
                best0 = jnp.full((rows, 1), NEG, F32)
            else:
                old = started(g, at)
                sums[g, at, :] = jnp.where(lane >= HD, old[:, HD : HD + 1], old)
                best0 = jnp.where(shifted, old[:, 2 * HD - 1 :], 0.0)
            own_ok = allowed(side, r) if first else None

            def one(index, best, q=q, g=g, at=at, own_ok=own_ok):
                base = pl.multiple_of(index * 512, 512)
                s = dot_nt(q, ks[pl.ds(base, 512), :]) * SCALE
                if own_ok is not None:
                    s = jnp.where(jnp.logical_or(own_ok, index > 0), s, NEG)
                new = jnp.maximum(best, jnp.max(s, axis=1, keepdims=True))
                p = jnp.exp(s - new)
                if own_ok is not None:
                    p = jnp.where(jnp.logical_or(own_ok, index > 0), p, 0.0)
                sums[g, at, :] = sums[g, at, :] * jnp.exp(best - new) + dot_nn(
                    p.astype(BF16), vx[pl.ds(base, 512), :]
                )
                return new

            best = lax.fori_loop(0, count, one, best0)
            if first:
                sums[g, at, :] = jnp.where(lane == 2 * HD - 1, best, sums[g, at, :])
            else:
                write(g, side, at, sums[g, at, :])


def prefill(meta, queries, q_oth, bufs, head, heads, before=None, group=4, rows=128):
    per = 16 // group
    at = head // group
    first = before is None
    steps = heads // group
    any_spec = pl.BlockSpec(memory_space=pl.ANY)
    smem = pl.BlockSpec(memory_space=pltpu.SMEM)
    state_shape = (group, 512, 2 * HD)
    in_specs = [
        pl.BlockSpec((256, group * HD), lambda i, m: (0, m[1] * per + at + i)),
        pl.BlockSpec((256, group * HD), lambda i, m: (0, at + i)),
    ] + [any_spec] * len(bufs)
    args = [queries, q_oth, *bufs]
    scratch = [pltpu.VMEM((2048, HD), BF16), pltpu.VMEM((2048, 2 * HD), BF16), pltpu.VMEM((8, HD), F32)]
    if first:
        out_specs = [pl.BlockSpec(state_shape, lambda i, m: (i, 0, 0)), smem]
        out_shape = [
            jax.ShapeDtypeStruct((heads,) + state_shape[1:], F32),
            jax.ShapeDtypeStruct((steps,), jnp.int32),
        ]
    else:
        (sums_a, flags_a), (sums_b, flags_b) = before
        split = sums_a.shape[0] // group
        in_specs += [
            pl.BlockSpec(state_shape, lambda i, m: (jnp.minimum(i, split - 1), 0, 0)),
            smem,
            pl.BlockSpec(state_shape, lambda i, m: (jnp.maximum(i - split, 0), 0, 0)),
            smem,
        ]
        args += [sums_a, flags_a, sums_b, flags_b]
        out_specs = [pl.BlockSpec((256, group * HD), lambda i, m: (0, i))] * 2
        out_shape = [jax.ShapeDtypeStruct((256, heads * HD), BF16)] * 2
        scratch.append(pltpu.VMEM(state_shape, F32))
    scratch.append(pltpu.SemaphoreType.DMA((4, 4)))
    return pl.pallas_call(
        functools.partial(prefill_kernel, group=group, rows=rows, first=first),
        grid_spec=pltpu.PrefetchScalarGridSpec(
            num_scalar_prefetch=1,
            grid=(steps,),
            in_specs=in_specs,
            out_specs=out_specs,
            scratch_shapes=scratch,
        ),
        out_shape=out_shape,
        compiler_params=pltpu.CompilerParams(vmem_limit_bytes=VMEM_LIMIT),
        cost_estimate=pl.CostEstimate(
            flops=8 * 512 * heads * 2048 * HD, bytes_accessed=4 * 2**20, transcendentals=0
        ),
        name="prefill_a" if first else "prefill_b",
    )(meta, *args)


def join_kernel(meta, *refs):
    parts, out, sem = refs[:-2], refs[-2], refs[-1]
    copies = []
    for side in range(2):
        at = (meta[1] if side == 0 else 1 - meta[1]) * 16 * HD
        for part in parts[side * len(parts) // 2 : (side + 1) * len(parts) // 2]:
            wide = part.shape[1]
            copies.append(
                pltpu.make_async_copy(part, out.at[:, pl.ds(pl.multiple_of(at, HD), wide)], sem.at[len(copies)])
            )
            at = at + wide
    for copy in copies:
        copy.start()
    for copy in copies:
        copy.wait()


def join(meta, own, oth):
    parts = [*own, *oth]
    return pl.pallas_call(
        join_kernel,
        grid_spec=pltpu.PrefetchScalarGridSpec(
            num_scalar_prefetch=1,
            grid=(1,),
            in_specs=[pl.BlockSpec(part.shape, lambda i, m: (0, 0)) for part in parts],
            out_specs=pl.BlockSpec(memory_space=pl.ANY),
            scratch_shapes=[pltpu.SemaphoreType.DMA((len(parts),))],
        ),
        out_shape=jax.ShapeDtypeStruct((256, 32 * HD), BF16),
        compiler_params=pltpu.CompilerParams(vmem_limit_bytes=SMALL_LIMIT),
        name="join",
    )(meta, *parts)


def decode_kernel(
    meta, table, q_ref, nk_ref, nv_ref, len_ref, own, f1, f2, f3, f4, b1, b2, b3,
    keep, send, ks, vx, sem,
):
    chip, core, zpos, mask = meta[0], meta[1], meta[4], meta[5]
    sources = {0: own, 7: f1, 6: f2, 5: f3, 4: f4, 1: b1, 2: b2, 3: b3}

    def page_copy(buf, off, page):
        return (
            pltpu.make_async_copy(
                buf.at[pl.ds(off, PAGE), :], ks.at[pl.ds(page * PAGE, PAGE), :], sem.at[page, 0]
            ),
            pltpu.make_async_copy(
                buf.at[pl.ds(off + 256, PAGE), :],
                vx.at[pl.ds(page * PAGE, PAGE), pl.ds(0, HD)],
                sem.at[page, 1],
            ),
        )

    for page in range(4):
        side, inner = page // 2, page % 2
        from_core = core if side == 0 else 1 - core
        prompt = table[zpos, chip * 4 + from_core * 2 + inner]
        rel = lax.rem(prompt - zpos + 8, 8)
        for r in range(8):
            buf, off = sources[r], side * 512 + inner * PAGE

            @pl.when(rel == r)
            def _start(buf=buf, off=off, page=page):
                for copy in page_copy(buf, off, page):
                    copy.start()

    vx[:, HD:] = jnp.ones((512 + 64, HD), BF16)
    ks[512:, :] = nk_ref[...].reshape(64, HD)
    vx[512:, :HD] = nv_ref[...].reshape(64, HD)
    for page in range(4):
        for copy in page_copy(own, 0, page):
            copy.wait()

    lens = len_ref[...]
    row = lax.broadcasted_iota(jnp.int32, (64, 64), 0)
    col = lax.broadcasted_iota(jnp.int32, (64, 64), 1)
    new_ok = (lax.rem(row, 16) == lax.rem(col, 16)) & (col <= row) & (chip == 0)
    pos = lax.broadcasted_iota(jnp.int32, (64, 256), 1)
    base = chip * 512
    ok0 = pos + (base + core * 256) < lens
    ok1 = pos + (base + (1 - core) * 256) < lens
    ok = jnp.concatenate([ok0, ok1, new_ok], axis=1)
    keys = ks[...]
    vals = vx[...]
    lane = lax.broadcasted_iota(jnp.int32, (64, HD), 1)
    for part, out in enumerate((keep, send)):
        stats = jnp.zeros((64, HD), F32)
        for g0 in range(0, 8, 4):
            qs = []
            for g in range(g0, g0 + 4):
                head = (part * 8 + g) ^ mask
                qs.append(q_ref[:, :, pl.ds(pl.multiple_of(head * HD, HD), HD)].reshape(64, HD))
            s = dot_nt(jnp.concatenate(qs, axis=0), keys) * SCALE
            s = jnp.where(jnp.concatenate([ok] * 4, axis=0), s, NEG)
            best = jnp.max(s, axis=1, keepdims=True).astype(BF16).astype(F32)
            p = jnp.exp(s - jnp.maximum(best, 0.5 * NEG)).astype(BF16)
            o = dot_nn(p, vals)
            for i in range(4):
                g = g0 + i
                at = slice(i * 64, (i + 1) * 64)
                out[:, g * HD : (g + 1) * HD] = o[at, :HD].astype(BF16)
                total = o[at, HD:]
                high = total.astype(BF16).astype(F32)
                stats = jnp.where(lane == g, best[at], stats)
                stats = jnp.where(lane == 16 + g, high, stats)
                stats = jnp.where(lane == 32 + g, total - high, stats)
        out[:, 8 * HD :] = stats.astype(BF16)


def decode_part(meta, table, dec_q, dec_k, dec_v, lens, bufs):
    any_spec = pl.BlockSpec(memory_space=pl.ANY)
    shape = jax.ShapeDtypeStruct((64, 9 * HD), BF16)
    return pl.pallas_call(
        decode_kernel,
        grid_spec=pltpu.PrefetchScalarGridSpec(
            num_scalar_prefetch=2,
            grid=(1,),
            in_specs=[
                pl.BlockSpec((4, 16, 16 * HD), lambda i, m, t: (0, 0, m[1])),
                pl.BlockSpec((4, 16, HD), lambda i, m, t: (0, 0, m[1])),
                pl.BlockSpec((4, 16, HD), lambda i, m, t: (0, 0, m[1])),
                pl.BlockSpec((64, 1), lambda i, m, t: (0, 0)),
            ]
            + [any_spec] * 8,
            out_specs=[pl.BlockSpec((64, 9 * HD), lambda i, m, t: (0, 0))] * 2,
            scratch_shapes=[
                pltpu.VMEM((512 + 64, HD), BF16),
                pltpu.VMEM((512 + 64, 2 * HD), BF16),
                pltpu.SemaphoreType.DMA((4, 2)),
            ],
        ),
        out_shape=[shape, shape],
        compiler_params=pltpu.CompilerParams(vmem_limit_bytes=SMALL_LIMIT),
        cost_estimate=pl.CostEstimate(flops=2 * 10**9, bytes_accessed=2**20, transcendentals=0),
        name="decode_part",
    )(meta, table, dec_q, dec_k, dec_v, lens, *bufs)


def merge_kernel(*refs, count, heads, last):
    ins, outs = refs[:count], refs[count:]
    cols = heads * HD
    lane = lax.broadcasted_iota(jnp.int32, (64, HD), 1)
    stats_in = [ref[:, cols:].astype(F32) for ref in ins]

    def total_of(stat):
        return pltpu.roll(stat, HD - 16, 1) + pltpu.roll(stat, HD - 32, 1)

    best = functools.reduce(jnp.maximum, stats_in)
    shares = [jnp.exp(stat - best) for stat in stats_in]
    total = sum(total_of(stat) * w for stat, w in zip(stats_in, shares))
    used = lane < heads
    if last:
        inverse = 1.0 / jnp.where(used, total, 1.0)
        shares = [w * inverse for w in shares]
    place = lax.broadcasted_iota(jnp.int32, (HD, cols), 0) == (
        lax.broadcasted_iota(jnp.int32, (HD, cols), 1) // HD
    )
    place = place.astype(BF16)

    def spread(w):
        w = jnp.where(used, w, 0.0)
        high = w.astype(BF16)
        low = (w - high.astype(F32)).astype(BF16)
        return dot_nn(high, place) + dot_nn(low, place)

    joined = sum(ref[:, :cols].astype(F32) * spread(w) for ref, w in zip(ins, shares))
    if last:
        outs[0][...] = joined.astype(BF16)
        return
    high = total.astype(BF16).astype(F32)
    low = total - high
    each = heads // len(outs)
    for part, out in enumerate(outs):
        first = part * each
        out[:, : each * HD] = joined[:, first * HD : (first + each) * HD].astype(BF16)
        stats = jnp.zeros((64, HD), F32)
        for values, goal in ((best, 0), (high, 16), (low, 32)):
            turn = (goal - first) % HD
            moved = pltpu.roll(values, turn, 1) if turn else values
            stats = jnp.where((lane >= goal) & (lane < goal + each), moved, stats)
        out[:, each * HD :] = stats.astype(BF16)


def merge(parts, heads, runs, last=False):
    width = heads * HD if last else (heads // runs + 1) * HD
    return pl.pallas_call(
        functools.partial(merge_kernel, count=len(parts), heads=heads, last=last),
        out_shape=[jax.ShapeDtypeStruct((64, width), BF16)] * runs,
        cost_estimate=pl.CostEstimate(flops=10**6, bytes_accessed=2**18, transcendentals=0),
        name="merge",
    )(*parts)


def place_kernel(meta, *refs):
    parts, out, sem = refs[:4], refs[4], refs[5]
    core, mask = meta[1], meta[5]
    copies = []
    for index, ref in enumerate(parts):
        which = core if index < 2 else 1 - core
        for b in range(4):
            at = pl.multiple_of((which * 16 + ((index % 2 * 8 + 2 * b) ^ mask)) * HD, 2 * HD)
            copies.append(
                pltpu.make_async_copy(
                    ref.at[:, :, b * 2 * HD : (b + 1) * 2 * HD], out.at[:, :, pl.ds(at, 2 * HD)], sem.at[index, b]
                )
            )
    for copy in copies:
        copy.start()
    for copy in copies:
        copy.wait()


def place(meta, parts):
    return pl.pallas_call(
        place_kernel,
        in_specs=[pl.BlockSpec(memory_space=pltpu.SMEM)] + [pl.BlockSpec(memory_space=pltpu.VMEM)] * 4,
        out_specs=pl.BlockSpec(memory_space=pl.ANY),
        scratch_shapes=[pltpu.SemaphoreType.DMA((4, 4))],
        out_shape=jax.ShapeDtypeStruct((4, 16, 4096), BF16),
        name="place",
    )(meta, *[part.reshape(4, 16, 1024) for part in parts])


def ctx_move(array, dx=0, flip_y=0, flip_core=0, mirror_x=0):
    pairs = []
    for c in range(16):
        x, y, core = c // 4, (c // 2) % 2, c % 2
        to_x = ((x + dx) % 4) ^ mirror_x
        pairs.append((c, to_x * 4 + (y ^ flip_y) * 2 + (core ^ flip_core)))
    return lax.ppermute(array, "ctx", pairs)


def dec_move(array, dz):
    return lax.ppermute(array, "dec", [(i, (i + dz) % 8) for i in range(8)])


def body(queries, keys, values, dec_queries, dec_keys, dec_values, page_table, ctx_lengths):
    c = lax.axis_index("ctx")
    z = lax.axis_index("dec")
    x, y, core = c // 4, (c // 2) % 2, c % 2
    chip = c // 2
    mask = y * 8 + x * 2
    meta = jnp.stack([chip, core, x, y, z, mask]).astype(jnp.int32)

    k0, v0 = keys[0], values[0]
    first = jnp.concatenate([k0[:, :HD], v0[:, :HD]], axis=0)
    second = jnp.concatenate([k0[:, HD:], v0[:, HD:]], axis=0)
    mine = jnp.where(core == 0, first, second)
    other = jnp.where(core == 0, second, first)
    q_send = lax.dynamic_slice_in_dim(queries[0], (1 - core) * 2048, 2048, 1)
    barrier = lax.optimization_barrier
    got, q_oth = barrier((ctx_move(other, flip_core=1), ctx_move(q_send, flip_core=1)))
    chunk = jnp.concatenate([mine, got], axis=0)
    lens = jnp.tile(ctx_lengths, 4)[:, None]

    q = queries[0]
    f1, b1 = dec_move(chunk, 1), dec_move(chunk, -1)
    rr, ll, yy = ctx_move(chunk, dx=1), ctx_move(chunk, dx=-1), ctx_move(chunk, flip_y=1)
    f1, b1, rr, ll, yy = barrier((f1, b1, rr, ll, yy))
    near = (chunk, rr, ll, yy)
    f2, b2 = dec_move(f1, 1), dec_move(b1, -1)
    ry, ly = ctx_move(yy, dx=1), ctx_move(yy, dx=-1)
    pa0 = prefill(meta, q, q_oth, near, 0, 8)
    f2, b2, ry, ly, pa0 = barrier((f2, b2, ry, ly, pa0))
    f3, b3, f4 = dec_move(f2, 1), dec_move(b2, -1), dec_move(f2, 2)
    xx, xy = ctx_move(rr, dx=1), ctx_move(ly, dx=-1)
    pa1 = prefill(meta, q, q_oth, near, 8, 8)
    f3, b3, f4, xx, xy, pa1 = barrier((f3, b3, f4, xx, xy, pa1))
    far = (ry, ly, xx, xy)

    keep, send = decode_part(
        meta, page_table, dec_queries, dec_keys, dec_values, lens, (chunk, f1, f2, f3, f4, b1, b2, b3)
    )
    got = ctx_move(send, flip_y=1)
    own_out, oth_out = prefill(meta, q, q_oth, far, 0, 16, (pa0, pa1))
    got, own_out, oth_out = barrier((got, own_out, oth_out))
    back = ctx_move(oth_out, flip_core=1)
    keep, *send = merge((keep, got), 8, 4)
    got = [ctx_move(send[k - 1], mirror_x=k) for k in (1, 2, 3)]
    got, back = barrier((got, back))
    (part,) = merge((keep, *got), 2, 1, last=True)
    got = [ctx_move(part, mirror_x=k) for k in (1, 2, 3)]
    prefill_out = join(meta, [own_out], [back])
    got, prefill_out = barrier((got, prefill_out))
    part = jnp.concatenate([part, *got], axis=1)
    decode_out = place(
        meta,
        [part, ctx_move(part, flip_y=1), ctx_move(part, flip_core=1), ctx_move(part, flip_y=1, flip_core=1)],
    )
    return (prefill_out[None], decode_out)


def solution(mesh):
    return jax.shard_map(
        body,
        mesh=mesh,
        in_specs=(
            P("dec", "ctx", "tp"),
            P("dec", "ctx", "tp"),
            P("dec", "ctx", "tp"),
            P(None, "dec", "tp"),
            P(None, "dec", "tp"),
            P(None, "dec", "tp"),
            P(),
            P("dec"),
        ),
        out_specs=(P("dec", "ctx", "tp"), P(None, "dec", "tp")),
        check_vma=False,
    )
```

```python
import functools

import jax
import jax.numpy as jnp
from jax import lax
from jax.experimental import pallas as pl
from jax.experimental.pallas import tpu as pltpu
from jax.sharding import PartitionSpec as P

HD = 128
PAGE = 128
SCALE = HD**-0.5
LOG2E = 1.4426950408889634
CEXP = SCALE * LOG2E
SAFE = 75.0
NEG = -1e30
NT = (((1,), (1,)), ((), ()))
VMEM_LIMIT = 56 * 2**20
SMALL_LIMIT = 16 * 2**20
F32 = jnp.float32
BF16 = jnp.bfloat16


def dot_nt(a, b):
    return lax.dot_general(a, b, NT, preferred_element_type=F32)


def dot_nn(a, b):
    return jnp.dot(a, b, preferred_element_type=F32)


def row_norm_bound(block, fold):
    sq = block.astype(F32)
    sq = sq * sq
    each = sq.shape[0] // fold
    most = sq[:each]
    for i in range(1, fold):
        most = jnp.maximum(most, sq[i * each : (i + 1) * each])
    return jnp.max(jnp.sum(most, axis=1, keepdims=True), axis=0, keepdims=True)


def prefill_kernel(meta, *refs, group, rows, first):
    chip, core, xpos, ypos = meta[0], meta[1], meta[2], meta[3]
    if first:
        q_own, q_oth, own, rr, ll, yy, state, flag, ks, vx, kbest, sem = refs
    else:
        q_own, q_oth, ry, ly, xx, xy, before_a, flag_a, before_b, flag_b = refs[:10]
        o_own, o_oth, ks, vx, kbest, acc, sem = refs[-7:]
    step = pl.program_id(0)
    half = 256

    def chip_id(dx, dy):
        return lax.rem(xpos + dx + 4, 4) * 2 + lax.rem(ypos + dy, 2)

    if first:
        pieces = [(chip_id(0, 0), own), (chip_id(-1, 0), rr), (chip_id(1, 0), ll), (chip_id(0, 1), yy)]
    else:
        pieces = [(chip_id(-1, 1), ry), (chip_id(1, 1), ly), (chip_id(2, 0), xx), (chip_id(2, 1), xy)]
    needed = [p[0] <= chip for p in pieces]
    slots, count = [], jnp.int32(0)
    for need in needed:
        slots.append(count)
        count = count + need.astype(jnp.int32)

    def copies(index):
        buf = pieces[index][1]
        base = slots[index] * 512
        out = []
        for side in range(2):
            off = side * 512
            dst = pl.multiple_of(base + side * half, half)
            out.append(
                pltpu.make_async_copy(
                    buf.at[pl.ds(off, half), :], ks.at[pl.ds(dst, half), :], sem.at[index, 2 * side]
                )
            )
            out.append(
                pltpu.make_async_copy(
                    buf.at[pl.ds(off + half, half), :],
                    vx.at[pl.ds(dst, half), pl.ds(0, HD)],
                    sem.at[index, 2 * side + 1],
                )
            )
        return out

    @pl.when(step == 0)
    def _load():
        for index in range(4):

            @pl.when(needed[index])
            def _start(index=index):
                for copy in copies(index):
                    copy.start()

        vx[:, HD:] = jnp.ones((vx.shape[0], HD), BF16)
        for index in range(4):

            @pl.when(needed[index])
            def _wait(index=index):
                for copy in copies(index):
                    copy.wait()

        def norm(block, best):
            return jnp.maximum(best, row_norm_bound(ks[pl.ds(pl.multiple_of(block * 512, 512), 512), :], 8))

        kbest[0:1, 0:1] = lax.fori_loop(0, count, norm, jnp.zeros((1, 1), F32))

    q_refs = (q_own, q_oth)
    qmax = jnp.zeros((1, 1), F32)
    for q_ref in q_refs:
        for g in range(group):
            qmax = jnp.maximum(qmax, row_norm_bound(q_ref[:, g * HD : (g + 1) * HD], 4))
    bound = qmax * kbest[0:1, 0:1] * (SCALE * SCALE * 1.0001)
    safe = bound[0, 0] <= SAFE * SAFE
    if first:
        flag[step] = jnp.where(safe, 0, 1)
    else:
        later = step >= flag_a.shape[0]
        shifted = jnp.where(later, flag_b[lax.rem(step, flag_b.shape[0])], flag_a[lax.rem(step, flag_a.shape[0])]) != 0
        safe = safe & jnp.logical_not(shifted)

    def tiles():
        for g in range(group):
            for side in range(2):
                for r in range(half // rows):
                    q = q_refs[side][r * rows : (r + 1) * rows, g * HD : (g + 1) * HD]
                    yield g, side, r, slice(side * half + r * rows, side * half + (r + 1) * rows), q

    def allowed(side, r):
        q_pos0 = (core if side == 0 else 1 - core) * half + r * rows
        row = lax.broadcasted_iota(jnp.int32, (rows, half), 0) + q_pos0
        col = lax.broadcasted_iota(jnp.int32, (rows, half), 1)
        return jnp.concatenate([col + core * half <= row, col + (1 - core) * half <= row], axis=1)

    def weighted(q, base, size, ok=None):
        p = jnp.exp2(dot_nt(q, ks[pl.ds(base, size), :]) * CEXP)
        if ok is not None:
            masked = jnp.where(ok, p[:, :512], 0.0)
            p = masked if size == 512 else jnp.concatenate([masked, p[:, 512:]], axis=1)
        return dot_nn(p.astype(BF16), vx[pl.ds(base, size), :])

    def write(g, side, at, both):
        cols = slice(g * HD, (g + 1) * HD)
        r = slice(at.start - side * half, at.stop - side * half)
        (o_own, o_oth)[side][r, cols] = (both[:, :HD] / both[:, HD:]).astype(BF16)

    full = count == 4

    def started(g, at):
        return jnp.where(later, before_b[g, at, :], before_a[g, at, :])


    @pl.when(safe & full)
    def _straight():
        for g, side, r, at, q in tiles():
            if first:
                state[g, at, :] = weighted(q, 0, 2048, allowed(side, r))
            else:
                write(g, side, at, started(g, at) + weighted(q, 0, 2048))

    @pl.when(safe & jnp.logical_not(full))
    def _plain():
        sums = state if first else acc
        for g, side, r, at, q in tiles():
            if first:
                sums[g, at, :] = weighted(q, 0, 512, allowed(side, r))
            else:
                sums[g, at, :] = started(g, at)

        def one(index, carry):
            for g, side, r, at, q in tiles():
                sums[g, at, :] += weighted(q, pl.multiple_of(index * 512, 512), 512)
            return carry

        lax.fori_loop(1 if first else 0, count, one, 0)
        if not first:
            for g, side, r, at, q in tiles():
                write(g, side, at, sums[g, at, :])

    @pl.when(jnp.logical_not(safe))
    def _online():
        sums = state if first else acc
        lane = lax.broadcasted_iota(jnp.int32, (rows, 2 * HD), 1)
        for side in range(2):

            def tile(number, carry, side=side):
                g, r = number // (half // rows), lax.rem(number, half // rows)
                q = q_refs[side][pl.ds(pl.multiple_of(r * rows, rows), rows), pl.ds(pl.multiple_of(g * HD, HD), HD)]
                at = pl.ds(pl.multiple_of(side * half + r * rows, rows), rows)
                if first:
                    sums[g, at, :] = jnp.zeros((rows, 2 * HD), F32)
                    best0 = jnp.full((rows, 1), NEG, F32)
                else:
                    old = started(g, at)
                    sums[g, at, :] = jnp.where(lane >= HD, old[:, HD : HD + 1], old)
                    best0 = jnp.where(shifted, old[:, 2 * HD - 1 :], 0.0)
                own_ok = allowed(side, r) if first else None

                def one(index, best):
                    base = pl.multiple_of(index * 512, 512)
                    s = dot_nt(q, ks[pl.ds(base, 512), :]) * SCALE
                    if own_ok is not None:
                        s = jnp.where(jnp.logical_or(own_ok, index > 0), s, NEG)
                    new = jnp.maximum(best, jnp.max(s, axis=1, keepdims=True))
                    p = jnp.exp(s - new)
                    if own_ok is not None:
                        p = jnp.where(jnp.logical_or(own_ok, index > 0), p, 0.0)
                    sums[g, at, :] = sums[g, at, :] * jnp.exp(best - new) + dot_nn(
                        p.astype(BF16), vx[pl.ds(base, 512), :]
                    )
                    return new

                best = lax.fori_loop(0, count, one, best0)
                both = sums[g, at, :]
                if first:
                    sums[g, at, :] = jnp.where(lane == 2 * HD - 1, best, both)
                else:
                    (o_own, o_oth)[side][
                        pl.ds(pl.multiple_of(r * rows, rows), rows), pl.ds(pl.multiple_of(g * HD, HD), HD)
                    ] = (both[:, :HD] / both[:, HD:]).astype(BF16)
                return carry

            lax.fori_loop(0, group * (half // rows), tile, 0)


def prefill(meta, queries, q_oth, bufs, head, heads, before=None, group=2, rows=128):
    per = 16 // group
    at = head // group
    first = before is None
    steps = heads // group
    any_spec = pl.BlockSpec(memory_space=pl.ANY)
    smem = pl.BlockSpec(memory_space=pltpu.SMEM)
    state_shape = (group, 512, 2 * HD)
    in_specs = [
        pl.BlockSpec((256, group * HD), lambda i, m: (0, m[1] * per + at + i)),
        pl.BlockSpec((256, group * HD), lambda i, m: (0, at + i)),
    ] + [any_spec] * len(bufs)
    args = [queries, q_oth, *bufs]
    scratch = [pltpu.VMEM((2048, HD), BF16), pltpu.VMEM((2048, 2 * HD), BF16), pltpu.VMEM((8, HD), F32)]
    if first:
        out_specs = [pl.BlockSpec(state_shape, lambda i, m: (i, 0, 0)), smem]
        out_shape = [
            jax.ShapeDtypeStruct((heads,) + state_shape[1:], F32),
            jax.ShapeDtypeStruct((steps,), jnp.int32),
        ]
    else:
        (sums_a, flags_a), (sums_b, flags_b) = before
        split = sums_a.shape[0] // group
        in_specs += [
            pl.BlockSpec(state_shape, lambda i, m: (jnp.minimum(i, split - 1), 0, 0)),
            smem,
            pl.BlockSpec(state_shape, lambda i, m: (jnp.maximum(i - split, 0), 0, 0)),
            smem,
        ]
        args += [sums_a, flags_a, sums_b, flags_b]
        out_specs = [pl.BlockSpec((256, group * HD), lambda i, m: (0, i))] * 2
        out_shape = [jax.ShapeDtypeStruct((256, heads * HD), BF16)] * 2
        scratch.append(pltpu.VMEM(state_shape, F32))
    scratch.append(pltpu.SemaphoreType.DMA((4, 4)))
    return pl.pallas_call(
        functools.partial(prefill_kernel, group=group, rows=rows, first=first),
        grid_spec=pltpu.PrefetchScalarGridSpec(
            num_scalar_prefetch=1,
            grid=(steps,),
            in_specs=in_specs,
            out_specs=out_specs,
            scratch_shapes=scratch,
        ),
        out_shape=out_shape,
        compiler_params=pltpu.CompilerParams(vmem_limit_bytes=VMEM_LIMIT),
        cost_estimate=pl.CostEstimate(
            flops=8 * 512 * heads * 2048 * HD, bytes_accessed=4 * 2**20, transcendentals=0
        ),
        name="prefill_a" if first else "prefill_b",
    )(meta, *args)


def join_kernel(meta, *refs):
    parts, out, sem = refs[:-2], refs[-2], refs[-1]
    copies = []
    for side in range(2):
        at = (meta[1] if side == 0 else 1 - meta[1]) * 16 * HD
        for part in parts[side * len(parts) // 2 : (side + 1) * len(parts) // 2]:
            wide = part.shape[1]
            copies.append(
                pltpu.make_async_copy(part, out.at[:, pl.ds(pl.multiple_of(at, HD), wide)], sem.at[len(copies)])
            )
            at = at + wide
    for copy in copies:
        copy.start()
    for copy in copies:
        copy.wait()


def join(meta, own, oth):
    parts = [*own, *oth]
    return pl.pallas_call(
        join_kernel,
        grid_spec=pltpu.PrefetchScalarGridSpec(
            num_scalar_prefetch=1,
            grid=(1,),
            in_specs=[pl.BlockSpec(part.shape, lambda i, m: (0, 0)) for part in parts],
            out_specs=pl.BlockSpec(memory_space=pl.ANY),
            scratch_shapes=[pltpu.SemaphoreType.DMA((len(parts),))],
        ),
        out_shape=jax.ShapeDtypeStruct((256, 32 * HD), BF16),
        compiler_params=pltpu.CompilerParams(vmem_limit_bytes=SMALL_LIMIT),
        name="join",
    )(meta, *parts)


def pick_kernel(meta, table, own, f1, b1, up, down):
    chip, core, z = meta[0], meta[1], meta[4]
    for out, shift in ((up, 3), (down, 5)):
        goal = lax.rem(z + shift, 8)
        for page in range(4):
            side, inner = page // 2, page % 2
            from_core = core if side == 0 else 1 - core
            rel = lax.rem(table[goal, chip * 4 + from_core * 2 + inner] - z + 8, 8)
            for kind in range(2):
                off = side * 512 + kind * 256 + inner * PAGE
                at = slice(off, off + PAGE)
                out[at, :] = jnp.where(rel == 1, b1[at, :], jnp.where(rel == 7, f1[at, :], own[at, :]))


def pick(meta, table, own, f1, b1):
    smem = pl.BlockSpec(memory_space=pltpu.SMEM)
    vmem = pl.BlockSpec(memory_space=pltpu.VMEM)
    return pl.pallas_call(
        pick_kernel,
        in_specs=[smem, smem, vmem, vmem, vmem],
        out_specs=[vmem, vmem],
        out_shape=[jax.ShapeDtypeStruct((1024, HD), BF16)] * 2,
        name="pick",
    )(meta, table, own, f1, b1)


def decode_kernel(
    meta, table, q_ref, nk_ref, nv_ref, len_ref, own, f1, b1, fs, bs,
    keep, send, ks, vx, sem,
):
    chip, core, zpos, mask = meta[0], meta[1], meta[4], meta[5]
    sources = {0: own, 7: f1, 1: b1, 2: bs, 3: bs, 4: fs, 5: fs, 6: fs}

    def page_copy(buf, off, page):
        return (
            pltpu.make_async_copy(
                buf.at[pl.ds(off, PAGE), :], ks.at[pl.ds(page * PAGE, PAGE), :], sem.at[page, 0]
            ),
            pltpu.make_async_copy(
                buf.at[pl.ds(off + 256, PAGE), :],
                vx.at[pl.ds(page * PAGE, PAGE), pl.ds(0, HD)],
                sem.at[page, 1],
            ),
        )

    for page in range(4):
        side, inner = page // 2, page % 2
        from_core = core if side == 0 else 1 - core
        prompt = table[zpos, chip * 4 + from_core * 2 + inner]
        rel = lax.rem(prompt - zpos + 8, 8)
        for r in range(8):
            buf, off = sources[r], side * 512 + inner * PAGE

            @pl.when(rel == r)
            def _start(buf=buf, off=off, page=page):
                for copy in page_copy(buf, off, page):
                    copy.start()

    vx[:, HD:] = jnp.ones((512 + 64, HD), BF16)
    ks[512:, :] = nk_ref[...].reshape(64, HD)
    vx[512:, :HD] = nv_ref[...].reshape(64, HD)
    for page in range(4):
        for copy in page_copy(own, 0, page):
            copy.wait()

    lens = len_ref[...]
    row = lax.broadcasted_iota(jnp.int32, (64, 64), 0)
    col = lax.broadcasted_iota(jnp.int32, (64, 64), 1)
    new_ok = (lax.rem(row, 16) == lax.rem(col, 16)) & (col <= row) & (chip == 0)
    pos = lax.broadcasted_iota(jnp.int32, (64, 256), 1)
    base = chip * 512
    ok0 = pos + (base + core * 256) < lens
    ok1 = pos + (base + (1 - core) * 256) < lens
    ok = jnp.concatenate([ok0, ok1, new_ok], axis=1)
    keys = ks[...]
    vals = vx[...]
    lane = lax.broadcasted_iota(jnp.int32, (64, HD), 1)
    for part, out in enumerate((keep, send)):
        stats = jnp.zeros((64, HD), F32)
        for g0 in range(0, 8, 4):
            qs = []
            for g in range(g0, g0 + 4):
                head = (part * 8 + g) ^ mask
                qs.append(q_ref[:, :, pl.ds(pl.multiple_of(head * HD, HD), HD)].reshape(64, HD))
            s = dot_nt(jnp.concatenate(qs, axis=0), keys) * SCALE
            s = jnp.where(jnp.concatenate([ok] * 4, axis=0), s, NEG)
            best = jnp.max(s, axis=1, keepdims=True).astype(BF16).astype(F32)
            p = jnp.exp(s - jnp.maximum(best, 0.5 * NEG)).astype(BF16)
            o = dot_nn(p, vals)
            for i in range(4):
                g = g0 + i
                at = slice(i * 64, (i + 1) * 64)
                out[:, g * HD : (g + 1) * HD] = o[at, :HD].astype(BF16)
                total = o[at, HD:]
                high = total.astype(BF16).astype(F32)
                stats = jnp.where(lane == g, best[at], stats)
                stats = jnp.where(lane == 16 + g, high, stats)
                stats = jnp.where(lane == 32 + g, total - high, stats)
        out[:, 8 * HD :] = stats.astype(BF16)


def decode_part(meta, table, dec_q, dec_k, dec_v, lens, bufs):
    any_spec = pl.BlockSpec(memory_space=pl.ANY)
    shape = jax.ShapeDtypeStruct((64, 9 * HD), BF16)
    return pl.pallas_call(
        decode_kernel,
        grid_spec=pltpu.PrefetchScalarGridSpec(
            num_scalar_prefetch=2,
            grid=(1,),
            in_specs=[
                pl.BlockSpec((4, 16, 16 * HD), lambda i, m, t: (0, 0, m[1])),
                pl.BlockSpec((4, 16, HD), lambda i, m, t: (0, 0, m[1])),
                pl.BlockSpec((4, 16, HD), lambda i, m, t: (0, 0, m[1])),
                pl.BlockSpec((64, 1), lambda i, m, t: (0, 0)),
            ]
            + [any_spec] * 5,
            out_specs=[pl.BlockSpec((64, 9 * HD), lambda i, m, t: (0, 0))] * 2,
            scratch_shapes=[
                pltpu.VMEM((512 + 64, HD), BF16),
                pltpu.VMEM((512 + 64, 2 * HD), BF16),
                pltpu.SemaphoreType.DMA((4, 2)),
            ],
        ),
        out_shape=[shape, shape],
        compiler_params=pltpu.CompilerParams(vmem_limit_bytes=SMALL_LIMIT),
        cost_estimate=pl.CostEstimate(flops=2 * 10**9, bytes_accessed=2**20, transcendentals=0),
        name="decode_part",
    )(meta, table, dec_q, dec_k, dec_v, lens, *bufs)


def merge_kernel(meta, *refs, count, heads, last):
    ins, out = refs[:count], refs[count]
    if last:
        held = refs[count + 1]
        for b in range(count):
            held[meta[2] ^ b] = ins[b][...]
        ins = [held.at[k] for k in range(count)]
    cols = heads * HD
    lane = lax.broadcasted_iota(jnp.int32, (64, HD), 1)
    stats_in = [ref[:, cols:].astype(F32) for ref in ins]

    def total_of(stat):
        return pltpu.roll(stat, HD - 16, 1) + pltpu.roll(stat, HD - 32, 1)

    best = functools.reduce(jnp.maximum, stats_in)
    shares = [jnp.exp(stat - best) for stat in stats_in]
    total = sum(total_of(stat) * w for stat, w in zip(stats_in, shares))
    used = lane < heads
    if last:
        inverse = 1.0 / jnp.where(used, total, 1.0)
        shares = [w * inverse for w in shares]
    place = lax.broadcasted_iota(jnp.int32, (HD, cols), 0) == (
        lax.broadcasted_iota(jnp.int32, (HD, cols), 1) // HD
    )
    place = place.astype(BF16)

    def spread(w):
        w = jnp.where(used, w, 0.0)
        high = w.astype(BF16)
        low = (w - high.astype(F32)).astype(BF16)
        return dot_nn(high, place) + dot_nn(low, place)

    joined = sum(ref[:, :cols].astype(F32) * spread(w) for ref, w in zip(ins, shares))
    out[:, :cols] = joined.astype(BF16)
    if last:
        return
    high = total.astype(BF16).astype(F32)
    stats = jnp.zeros((64, HD), F32)
    for values, goal in ((best, 0), (high, 16), (total - high, 32)):
        moved = pltpu.roll(values, goal, 1) if goal else values
        stats = jnp.where((lane >= goal) & (lane < goal + heads), moved, stats)
    out[:, cols:] = stats.astype(BF16)


def merge(meta, parts, heads, last=False):
    width = heads * HD if last else (heads + 1) * HD
    vmem = pl.BlockSpec(memory_space=pltpu.VMEM)
    return pl.pallas_call(
        functools.partial(merge_kernel, count=len(parts), heads=heads, last=last),
        in_specs=[pl.BlockSpec(memory_space=pltpu.SMEM)] + [vmem] * len(parts),
        out_specs=vmem,
        scratch_shapes=[pltpu.VMEM((len(parts), 64, (heads + 1) * HD), BF16)] if last else [],
        out_shape=jax.ShapeDtypeStruct((64, width), BF16),
        cost_estimate=pl.CostEstimate(flops=10**6, bytes_accessed=2**18, transcendentals=0),
        name="merge",
    )(meta, *parts)


def place_kernel(meta, *refs):
    parts, out, sem = refs[:4], refs[4], refs[5]
    core, mask = meta[1], meta[5]
    copies = []
    for index, ref in enumerate(parts):
        which = core if index < 2 else 1 - core
        for b in range(4):
            at = pl.multiple_of((which * 16 + ((index % 2 * 8 + 2 * b) ^ mask)) * HD, 2 * HD)
            copies.append(
                pltpu.make_async_copy(
                    ref.at[:, :, b * 2 * HD : (b + 1) * 2 * HD], out.at[:, :, pl.ds(at, 2 * HD)], sem.at[index, b]
                )
            )
    for copy in copies:
        copy.start()
    for copy in copies:
        copy.wait()


def place(meta, parts):
    return pl.pallas_call(
        place_kernel,
        in_specs=[pl.BlockSpec(memory_space=pltpu.SMEM)] + [pl.BlockSpec(memory_space=pltpu.VMEM)] * 4,
        out_specs=pl.BlockSpec(memory_space=pl.ANY),
        scratch_shapes=[pltpu.SemaphoreType.DMA((4, 4))],
        out_shape=jax.ShapeDtypeStruct((4, 16, 4096), BF16),
        name="place",
    )(meta, *[part.reshape(4, 16, 1024) for part in parts])


def ctx_move(array, dx=0, flip_y=0, flip_core=0, mirror_x=0):
    pairs = []
    for c in range(16):
        x, y, core = c // 4, (c // 2) % 2, c % 2
        to_x = ((x + dx) % 4) ^ mirror_x
        pairs.append((c, to_x * 4 + (y ^ flip_y) * 2 + (core ^ flip_core)))
    return lax.ppermute(array, "ctx", pairs)


def dec_move(array, dz):
    return lax.ppermute(array, "dec", [(i, (i + dz) % 8) for i in range(8)])


def body(queries, keys, values, dec_queries, dec_keys, dec_values, page_table, ctx_lengths):
    c = lax.axis_index("ctx")
    z = lax.axis_index("dec")
    x, y, core = c // 4, (c // 2) % 2, c % 2
    chip = c // 2
    mask = y * 8
    meta = jnp.stack([chip, core, x, y, z, mask]).astype(jnp.int32)

    k0, v0 = keys[0], values[0]
    first = jnp.concatenate([k0[:, :HD], v0[:, :HD]], axis=0)
    second = jnp.concatenate([k0[:, HD:], v0[:, HD:]], axis=0)
    mine = jnp.where(core == 0, first, second)
    other = jnp.where(core == 0, second, first)
    barrier = lax.optimization_barrier
    q, other = barrier((queries[0], other))
    got = ctx_move(other, flip_core=1)
    q_oth = ctx_move(lax.dynamic_slice_in_dim(q, (1 - core) * 2048, 2048, 1), flip_core=1)
    got, q_oth, meta = barrier((got, q_oth, meta))
    chunk = jnp.concatenate([mine, got], axis=0)
    lens = jnp.tile(ctx_lengths, 4)[:, None]
    f1, b1 = dec_move(chunk, 1), dec_move(chunk, -1)
    rr, ll, yy = ctx_move(chunk, dx=1), ctx_move(chunk, dx=-1), ctx_move(chunk, flip_y=1)
    f1, b1, rr, ll, yy, lens = barrier((f1, b1, rr, ll, yy, lens))
    near = (chunk, rr, ll, yy)
    up, down = pick(meta, page_table, chunk, f1, b1)
    fs, bs = dec_move(up, 3), dec_move(down, -3)
    ry, ly, xx = ctx_move(yy, dx=1), ctx_move(yy, dx=-1), ctx_move(rr, dx=1)
    pa0 = prefill(meta, q, q_oth, near, 0, 8)
    ry, ly, xx, fs, bs, pa0 = barrier((ry, ly, xx, fs, bs, pa0))
    keep, send = decode_part(
        meta, page_table, dec_queries, dec_keys, dec_values, lens, (chunk, f1, b1, fs, bs)
    )
    send, meta = barrier((send, meta))
    got = ctx_move(send, flip_y=1)
    xy = ctx_move(ly, dx=-1)
    pa1 = prefill(meta, q, q_oth, near, 8, 8)
    got, xy, pa1 = barrier((got, xy, pa1))
    part = merge(meta, (keep, got), 8)
    part, meta = barrier((part, meta))
    got = [ctx_move(part, mirror_x=k) for k in (1, 2, 3)]
    own_out, oth_out = prefill(meta, q, q_oth, (ry, ly, xx, xy), 0, 16, (pa0, pa1))
    got, own_out, oth_out = barrier((got, own_out, oth_out))
    back = ctx_move(oth_out, flip_core=1)
    part = merge(meta, (part, *got), 8, last=True)
    part, back = barrier((part, back))
    got = [ctx_move(part, flip_y=1), ctx_move(part, flip_core=1), ctx_move(part, flip_y=1, flip_core=1)]
    prefill_out = join(meta, [own_out], [back])
    got, prefill_out = barrier((got, prefill_out))
    decode_out = place(meta, [part, *got])
    return (prefill_out[None], decode_out)


def solution(mesh):
    return jax.shard_map(
        body,
        mesh=mesh,
        in_specs=(
            P("dec", "ctx", "tp"),
            P("dec", "ctx", "tp"),
            P("dec", "ctx", "tp"),
            P(None, "dec", "tp"),
            P(None, "dec", "tp"),
            P(None, "dec", "tp"),
            P(),
            P("dec"),
        ),
        out_specs=(P("dec", "ctx", "tp"), P(None, "dec", "tp")),
        check_vma=False,
    )
```

```python
import functools

import jax
import jax.numpy as jnp
from jax import lax
from jax.experimental import pallas as pl
from jax.experimental.pallas import tpu as pltpu
from jax.sharding import PartitionSpec as P

HD = 128
PAGE = 128
SCALE = HD**-0.5
LOG2E = 1.4426950408889634
CEXP = SCALE * LOG2E
SAFE = 75.0
NEG = -1e30
NT = (((1,), (1,)), ((), ()))
VMEM_LIMIT = 56 * 2**20
SMALL_LIMIT = 16 * 2**20
F32 = jnp.float32
BF16 = jnp.bfloat16


def dot_nt(a, b):
    return lax.dot_general(a, b, NT, preferred_element_type=F32)


def dot_nn(a, b):
    return jnp.dot(a, b, preferred_element_type=F32)


def row_norm_bound(block, fold):
    sq = block.astype(F32)
    sq = sq * sq
    each = sq.shape[0] // fold
    most = sq[:each]
    for i in range(1, fold):
        most = jnp.maximum(most, sq[i * each : (i + 1) * each])
    return jnp.max(jnp.sum(most, axis=1, keepdims=True), axis=0, keepdims=True)


def prefill_kernel(meta, *refs, group, rows, first):
    chip, core, xpos, ypos = meta[0], meta[1], meta[2], meta[3]
    if first:
        q_own, q_oth, own, rr, ll, yy, state, flag, ks, vx, kbest, sem = refs
    else:
        q_own, q_oth, yrl, xx, xy, before_a, flag_a, before_b, flag_b = refs[:9]
        o_own, o_oth, ks, vx, kbest, acc, sem = refs[-7:]
    step = pl.program_id(0)
    half = 256

    def chip_id(dx, dy):
        return lax.rem(xpos + dx + 4, 4) * 2 + lax.rem(ypos + dy, 2)

    if first:
        pieces = [(chip_id(0, 0), own, 0), (chip_id(-1, 0), rr, 0), (chip_id(1, 0), ll, 0), (chip_id(0, 1), yy, 0)]
    else:
        pieces = [(chip_id(-1, 1), yrl, 0), (chip_id(1, 1), yrl, 1024), (chip_id(2, 0), xx, 0), (chip_id(2, 1), xy, 0)]
    needed = [p[0] <= chip for p in pieces]
    slots, count = [], jnp.int32(0)
    for need in needed:
        slots.append(count)
        count = count + need.astype(jnp.int32)

    def copies(index):
        _, buf, start = pieces[index]
        base = slots[index] * 512
        out = []
        for side in range(2):
            off = start + side * 512
            dst = pl.multiple_of(base + side * half, half)
            out.append(
                pltpu.make_async_copy(
                    buf.at[pl.ds(off, half), :], ks.at[pl.ds(dst, half), :], sem.at[index, 2 * side]
                )
            )
            out.append(
                pltpu.make_async_copy(
                    buf.at[pl.ds(off + half, half), :],
                    vx.at[pl.ds(dst, half), pl.ds(0, HD)],
                    sem.at[index, 2 * side + 1],
                )
            )
        return out

    @pl.when(step == 0)
    def _load():
        for index in range(4):

            @pl.when(needed[index])
            def _start(index=index):
                for copy in copies(index):
                    copy.start()

        vx[:, HD:] = jnp.ones((vx.shape[0], HD), BF16)
        for index in range(4):

            @pl.when(needed[index])
            def _wait(index=index):
                for copy in copies(index):
                    copy.wait()

        def norm(block, best):
            return jnp.maximum(best, row_norm_bound(ks[pl.ds(pl.multiple_of(block * 512, 512), 512), :], 8))

        kbest[0:1, 0:1] = lax.fori_loop(0, count, norm, jnp.zeros((1, 1), F32))

    q_refs = (q_own, q_oth)
    qmax = jnp.zeros((1, 1), F32)
    for q_ref in q_refs:
        for g in range(group):
            qmax = jnp.maximum(qmax, row_norm_bound(q_ref[:, g * HD : (g + 1) * HD], 4))
    bound = qmax * kbest[0:1, 0:1] * (SCALE * SCALE * 1.0001)
    safe = bound[0, 0] <= SAFE * SAFE
    if first:
        flag[step] = jnp.where(safe, 0, 1)
    else:
        later = step >= flag_a.shape[0]
        shifted = jnp.where(later, flag_b[lax.rem(step, flag_b.shape[0])], flag_a[lax.rem(step, flag_a.shape[0])]) != 0
        safe = safe & jnp.logical_not(shifted)

    def tiles():
        for g in range(group):
            for side in range(2):
                for r in range(half // rows):
                    q = q_refs[side][r * rows : (r + 1) * rows, g * HD : (g + 1) * HD]
                    yield g, side, r, slice(side * half + r * rows, side * half + (r + 1) * rows), q

    def allowed(side, r):
        q_pos0 = (core if side == 0 else 1 - core) * half + r * rows
        row = lax.broadcasted_iota(jnp.int32, (rows, half), 0) + q_pos0
        col = lax.broadcasted_iota(jnp.int32, (rows, half), 1)
        return jnp.concatenate([col + core * half <= row, col + (1 - core) * half <= row], axis=1)

    def weighted(q, base, size, ok=None):
        p = jnp.exp2(dot_nt(q, ks[pl.ds(base, size), :]) * CEXP)
        if ok is not None:
            masked = jnp.where(ok, p[:, :512], 0.0)
            p = masked if size == 512 else jnp.concatenate([masked, p[:, 512:]], axis=1)
        return dot_nn(p.astype(BF16), vx[pl.ds(base, size), :])

    def write(g, side, at, both):
        cols = slice(g * HD, (g + 1) * HD)
        r = slice(at.start - side * half, at.stop - side * half)
        (o_own, o_oth)[side][r, cols] = (both[:, :HD] / both[:, HD:]).astype(BF16)

    full = count == 4

    def started(g, at):
        return jnp.where(later, before_b[g, at, :], before_a[g, at, :])


    @pl.when(safe & full)
    def _straight():
        for g, side, r, at, q in tiles():
            if first:
                state[g, at, :] = weighted(q, 0, 2048, allowed(side, r))
            else:
                write(g, side, at, started(g, at) + weighted(q, 0, 2048))

    @pl.when(safe & jnp.logical_not(full))
    def _plain():
        sums = state if first else acc
        for g, side, r, at, q in tiles():
            if first:
                sums[g, at, :] = weighted(q, 0, 512, allowed(side, r))
            else:
                sums[g, at, :] = started(g, at)

        def one(index, carry):
            for g, side, r, at, q in tiles():
                sums[g, at, :] += weighted(q, pl.multiple_of(index * 512, 512), 512)
            return carry

        lax.fori_loop(1 if first else 0, count, one, 0)
        if not first:
            for g, side, r, at, q in tiles():
                write(g, side, at, sums[g, at, :])

    @pl.when(jnp.logical_not(safe))
    def _online():
        sums = state if first else acc
        lane = lax.broadcasted_iota(jnp.int32, (rows, 2 * HD), 1)
        for side in range(2):

            def tile(number, carry, side=side):
                g, r = number // (half // rows), lax.rem(number, half // rows)
                q = q_refs[side][pl.ds(pl.multiple_of(r * rows, rows), rows), pl.ds(pl.multiple_of(g * HD, HD), HD)]
                at = pl.ds(pl.multiple_of(side * half + r * rows, rows), rows)
                if first:
                    sums[g, at, :] = jnp.zeros((rows, 2 * HD), F32)
                    best0 = jnp.full((rows, 1), NEG, F32)
                else:
                    old = started(g, at)
                    sums[g, at, :] = jnp.where(lane >= HD, old[:, HD : HD + 1], old)
                    best0 = jnp.where(shifted, old[:, 2 * HD - 1 :], 0.0)
                own_ok = allowed(side, r) if first else None

                def one(index, best):
                    base = pl.multiple_of(index * 512, 512)
                    s = dot_nt(q, ks[pl.ds(base, 512), :]) * SCALE
                    if own_ok is not None:
                        s = jnp.where(jnp.logical_or(own_ok, index > 0), s, NEG)
                    new = jnp.maximum(best, jnp.max(s, axis=1, keepdims=True))
                    p = jnp.exp(s - new)
                    if own_ok is not None:
                        p = jnp.where(jnp.logical_or(own_ok, index > 0), p, 0.0)
                    sums[g, at, :] = sums[g, at, :] * jnp.exp(best - new) + dot_nn(
                        p.astype(BF16), vx[pl.ds(base, 512), :]
                    )
                    return new

                best = lax.fori_loop(0, count, one, best0)
                both = sums[g, at, :]
                if first:
                    sums[g, at, :] = jnp.where(lane == 2 * HD - 1, best, both)
                else:
                    (o_own, o_oth)[side][
                        pl.ds(pl.multiple_of(r * rows, rows), rows), pl.ds(pl.multiple_of(g * HD, HD), HD)
                    ] = (both[:, :HD] / both[:, HD:]).astype(BF16)
                return carry

            lax.fori_loop(0, group * (half // rows), tile, 0)


def prefill(meta, queries, q_oth, bufs, head, heads, before=None, group=2, rows=128):
    per = 16 // group
    at = head // group
    first = before is None
    steps = heads // group
    any_spec = pl.BlockSpec(memory_space=pl.ANY)
    smem = pl.BlockSpec(memory_space=pltpu.SMEM)
    state_shape = (group, 512, 2 * HD)
    in_specs = [
        pl.BlockSpec((256, group * HD), lambda i, m: (0, m[1] * per + at + i)),
        pl.BlockSpec((256, group * HD), lambda i, m: (0, at + i)),
    ] + [any_spec] * len(bufs)
    args = [queries, q_oth, *bufs]
    scratch = [pltpu.VMEM((2048, HD), BF16), pltpu.VMEM((2048, 2 * HD), BF16), pltpu.VMEM((8, HD), F32)]
    if first:
        out_specs = [pl.BlockSpec(state_shape, lambda i, m: (i, 0, 0)), smem]
        out_shape = [
            jax.ShapeDtypeStruct((heads,) + state_shape[1:], F32),
            jax.ShapeDtypeStruct((steps,), jnp.int32),
        ]
    else:
        (sums_a, flags_a), (sums_b, flags_b) = before
        split = sums_a.shape[0] // group
        in_specs += [
            pl.BlockSpec(state_shape, lambda i, m: (jnp.minimum(i, split - 1), 0, 0)),
            smem,
            pl.BlockSpec(state_shape, lambda i, m: (jnp.maximum(i - split, 0), 0, 0)),
            smem,
        ]
        args += [sums_a, flags_a, sums_b, flags_b]
        out_specs = [pl.BlockSpec((256, group * HD), lambda i, m: (0, i))] * 2
        out_shape = [jax.ShapeDtypeStruct((256, heads * HD), BF16)] * 2
        scratch.append(pltpu.VMEM(state_shape, F32))
    scratch.append(pltpu.SemaphoreType.DMA((4, 4)))
    return pl.pallas_call(
        functools.partial(prefill_kernel, group=group, rows=rows, first=first),
        grid_spec=pltpu.PrefetchScalarGridSpec(
            num_scalar_prefetch=1,
            grid=(steps,),
            in_specs=in_specs,
            out_specs=out_specs,
            scratch_shapes=scratch,
        ),
        out_shape=out_shape,
        compiler_params=pltpu.CompilerParams(vmem_limit_bytes=VMEM_LIMIT),
        cost_estimate=pl.CostEstimate(
            flops=8 * 512 * heads * 2048 * HD, bytes_accessed=4 * 2**20, transcendentals=0
        ),
        name="prefill_a" if first else "prefill_b",
    )(meta, *args)


def join_kernel(meta, *refs):
    parts, out, sem = refs[:-2], refs[-2], refs[-1]
    copies = []
    for side in range(2):
        at = (meta[1] if side == 0 else 1 - meta[1]) * 16 * HD
        for part in parts[side * len(parts) // 2 : (side + 1) * len(parts) // 2]:
            wide = part.shape[1]
            copies.append(
                pltpu.make_async_copy(part, out.at[:, pl.ds(pl.multiple_of(at, HD), wide)], sem.at[len(copies)])
            )
            at = at + wide
    for copy in copies:
        copy.start()
    for copy in copies:
        copy.wait()


def join(meta, own, oth):
    parts = [*own, *oth]
    return pl.pallas_call(
        join_kernel,
        grid_spec=pltpu.PrefetchScalarGridSpec(
            num_scalar_prefetch=1,
            grid=(1,),
            in_specs=[pl.BlockSpec(part.shape, lambda i, m: (0, 0)) for part in parts],
            out_specs=pl.BlockSpec(memory_space=pl.ANY),
            scratch_shapes=[pltpu.SemaphoreType.DMA((len(parts),))],
        ),
        out_shape=jax.ShapeDtypeStruct((256, 32 * HD), BF16),
        compiler_params=pltpu.CompilerParams(vmem_limit_bytes=SMALL_LIMIT),
        name="join",
    )(meta, *parts)


def pick_kernel(meta, table, own, f1, b1, rr, ll, up, down, both):
    both[:1024, :] = rr[...]
    both[1024:, :] = ll[...]
    chip, core, z = meta[0], meta[1], meta[4]
    for out, shift in ((up, 3), (down, 5)):
        goal = lax.rem(z + shift, 8)
        for page in range(4):
            side, inner = page // 2, page % 2
            from_core = core if side == 0 else 1 - core
            rel = lax.rem(table[goal, chip * 4 + from_core * 2 + inner] - z + 8, 8)
            for kind in range(2):
                off = side * 512 + kind * 256 + inner * PAGE
                at = slice(off, off + PAGE)
                out[at, :] = jnp.where(rel == 1, b1[at, :], jnp.where(rel == 7, f1[at, :], own[at, :]))


def pick(meta, table, own, f1, b1, rr, ll):
    smem = pl.BlockSpec(memory_space=pltpu.SMEM)
    vmem = pl.BlockSpec(memory_space=pltpu.VMEM)
    return pl.pallas_call(
        pick_kernel,
        in_specs=[smem, smem] + [vmem] * 5,
        out_specs=[vmem] * 3,
        out_shape=[jax.ShapeDtypeStruct((n, HD), BF16) for n in (1024, 1024, 2048)],
        compiler_params=pltpu.CompilerParams(vmem_limit_bytes=SMALL_LIMIT),
        name="pick",
    )(meta, table, own, f1, b1, rr, ll)


def decode_kernel(
    meta, table, q_ref, nk_ref, nv_ref, len_ref, own, f1, b1, fs, bs,
    out, ks, vx, sem,
):
    chip, core, zpos = meta[0], meta[1], meta[4]
    sources = {0: own, 7: f1, 1: b1, 2: bs, 3: bs, 4: fs, 5: fs, 6: fs}

    def page_copy(buf, off, page):
        return (
            pltpu.make_async_copy(
                buf.at[pl.ds(off, PAGE), :], ks.at[pl.ds(page * PAGE, PAGE), :], sem.at[page, 0]
            ),
            pltpu.make_async_copy(
                buf.at[pl.ds(off + 256, PAGE), :],
                vx.at[pl.ds(page * PAGE, PAGE), pl.ds(0, HD)],
                sem.at[page, 1],
            ),
        )

    for page in range(4):
        side, inner = page // 2, page % 2
        from_core = core if side == 0 else 1 - core
        prompt = table[zpos, chip * 4 + from_core * 2 + inner]
        rel = lax.rem(prompt - zpos + 8, 8)
        for r in range(8):
            buf, off = sources[r], side * 512 + inner * PAGE

            @pl.when(rel == r)
            def _start(buf=buf, off=off, page=page):
                for copy in page_copy(buf, off, page):
                    copy.start()

    vx[:, HD:] = jnp.ones((512 + 64, HD), BF16)
    ks[512:, :] = nk_ref[...].reshape(64, HD)
    vx[512:, :HD] = nv_ref[...].reshape(64, HD)
    for page in range(4):
        for copy in page_copy(own, 0, page):
            copy.wait()

    lens = len_ref[...]
    row = lax.broadcasted_iota(jnp.int32, (64, 64), 0)
    col = lax.broadcasted_iota(jnp.int32, (64, 64), 1)
    new_ok = (lax.rem(row, 16) == lax.rem(col, 16)) & (col <= row) & (chip == 0)
    pos = lax.broadcasted_iota(jnp.int32, (64, 256), 1)
    base = chip * 512
    ok0 = pos + (base + core * 256) < lens
    ok1 = pos + (base + (1 - core) * 256) < lens
    ok = jnp.concatenate([ok0, ok1, new_ok], axis=1)
    keys = ks[...]
    vals = vx[...]
    lane = lax.broadcasted_iota(jnp.int32, (64, HD), 1)
    stats = jnp.zeros((64, HD), F32)
    for g0 in range(0, 16, 4):
        qs = [q_ref[:, :, h * HD : (h + 1) * HD].reshape(64, HD) for h in range(g0, g0 + 4)]
        s = dot_nt(jnp.concatenate(qs, axis=0), keys) * SCALE
        s = jnp.where(jnp.concatenate([ok] * 4, axis=0), s, NEG)
        best = jnp.max(s, axis=1, keepdims=True).astype(BF16).astype(F32)
        p = jnp.exp(s - jnp.maximum(best, 0.5 * NEG)).astype(BF16)
        o = dot_nn(p, vals)
        for i in range(4):
            h = g0 + i
            at = slice(i * 64, (i + 1) * 64)
            out[:, h * HD : (h + 1) * HD] = o[at, :HD].astype(BF16)
            total = o[at, HD:]
            high = total.astype(BF16).astype(F32)
            stats = jnp.where(lane == h, best[at], stats)
            stats = jnp.where(lane == 16 + h, high, stats)
            stats = jnp.where(lane == 32 + h, total - high, stats)
    out[:, 16 * HD :] = stats.astype(BF16)


def decode_part(meta, table, dec_q, dec_k, dec_v, lens, bufs):
    any_spec = pl.BlockSpec(memory_space=pl.ANY)
    return pl.pallas_call(
        decode_kernel,
        grid_spec=pltpu.PrefetchScalarGridSpec(
            num_scalar_prefetch=2,
            grid=(1,),
            in_specs=[
                pl.BlockSpec((4, 16, 16 * HD), lambda i, m, t: (0, 0, m[1])),
                pl.BlockSpec((4, 16, HD), lambda i, m, t: (0, 0, m[1])),
                pl.BlockSpec((4, 16, HD), lambda i, m, t: (0, 0, m[1])),
                pl.BlockSpec((64, 1), lambda i, m, t: (0, 0)),
            ]
            + [any_spec] * 5,
            out_specs=pl.BlockSpec((64, 17 * HD), lambda i, m, t: (0, 0)),
            scratch_shapes=[
                pltpu.VMEM((512 + 64, HD), BF16),
                pltpu.VMEM((512 + 64, 2 * HD), BF16),
                pltpu.SemaphoreType.DMA((4, 2)),
            ],
        ),
        out_shape=jax.ShapeDtypeStruct((64, 17 * HD), BF16),
        compiler_params=pltpu.CompilerParams(vmem_limit_bytes=SMALL_LIMIT),
        cost_estimate=pl.CostEstimate(flops=2 * 10**9, bytes_accessed=2**20, transcendentals=0),
        name="decode_part",
    )(meta, table, dec_q, dec_k, dec_v, lens, *bufs)


def merge_kernel(meta, *refs, axis, count, heads, last):
    ins, out, held = refs[:count], refs[count], refs[count + 1]
    for b in range(count):
        held[meta[axis] ^ b] = ins[b][...]
    ins = [held.at[k] for k in range(count)]
    cols = heads * HD
    lane = lax.broadcasted_iota(jnp.int32, (64, HD), 1)
    stats_in = [ref[:, cols:].astype(F32) for ref in ins]

    def total_of(stat):
        return pltpu.roll(stat, HD - 16, 1) + pltpu.roll(stat, HD - 32, 1)

    best = functools.reduce(jnp.maximum, stats_in)
    shares = [jnp.exp(stat - best) for stat in stats_in]
    total = sum(total_of(stat) * w for stat, w in zip(stats_in, shares))
    used = lane < heads
    if last:
        inverse = 1.0 / jnp.where(used, total, 1.0)
        shares = [w * inverse for w in shares]
    place = lax.broadcasted_iota(jnp.int32, (HD, cols), 0) == (
        lax.broadcasted_iota(jnp.int32, (HD, cols), 1) // HD
    )
    place = place.astype(BF16)

    def spread(w):
        w = jnp.where(used, w, 0.0)
        high = w.astype(BF16)
        low = (w - high.astype(F32)).astype(BF16)
        return dot_nn(high, place) + dot_nn(low, place)

    joined = sum(ref[:, :cols].astype(F32) * spread(w) for ref, w in zip(ins, shares))
    out[:, :cols] = joined.astype(BF16)
    if last:
        return
    high = total.astype(BF16).astype(F32)
    stats = jnp.zeros((64, HD), F32)
    for values, goal in ((best, 0), (high, 16), (total - high, 32)):
        moved = pltpu.roll(values, goal, 1) if goal else values
        stats = jnp.where((lane >= goal) & (lane < goal + heads), moved, stats)
    out[:, cols:] = stats.astype(BF16)


def merge(meta, parts, axis, heads=16, last=False):
    width = heads * HD if last else (heads + 1) * HD
    vmem = pl.BlockSpec(memory_space=pltpu.VMEM)
    return pl.pallas_call(
        functools.partial(merge_kernel, axis=axis, count=len(parts), heads=heads, last=last),
        in_specs=[pl.BlockSpec(memory_space=pltpu.SMEM)] + [vmem] * len(parts),
        out_specs=vmem,
        scratch_shapes=[pltpu.VMEM((len(parts), 64, (heads + 1) * HD), BF16)],
        out_shape=jax.ShapeDtypeStruct((64, width), BF16),
        compiler_params=pltpu.CompilerParams(vmem_limit_bytes=SMALL_LIMIT),
        cost_estimate=pl.CostEstimate(flops=10**6, bytes_accessed=2**18, transcendentals=0),
        name="merge",
    )(meta, *parts)


def place_kernel(meta, own, oth, out, sem):
    copies = []
    for side, ref in enumerate((own, oth)):
        at = pl.multiple_of((meta[1] if side == 0 else 1 - meta[1]) * 16 * HD, 16 * HD)
        copies.append(pltpu.make_async_copy(ref, out.at[:, :, pl.ds(at, 16 * HD)], sem.at[side]))
    for copy in copies:
        copy.start()
    for copy in copies:
        copy.wait()


def place(meta, own, oth):
    return pl.pallas_call(
        place_kernel,
        in_specs=[pl.BlockSpec(memory_space=pltpu.SMEM)] + [pl.BlockSpec(memory_space=pltpu.VMEM)] * 2,
        out_specs=pl.BlockSpec(memory_space=pl.ANY),
        scratch_shapes=[pltpu.SemaphoreType.DMA((2,))],
        out_shape=jax.ShapeDtypeStruct((4, 16, 4096), BF16),
        name="place",
    )(meta, own.reshape(4, 16, 2048), oth.reshape(4, 16, 2048))


def ctx_move(array, dx=0, flip_y=0, flip_core=0, mirror_x=0):
    pairs = []
    for c in range(16):
        x, y, core = c // 4, (c // 2) % 2, c % 2
        to_x = ((x + dx) % 4) ^ mirror_x
        pairs.append((c, to_x * 4 + (y ^ flip_y) * 2 + (core ^ flip_core)))
    return lax.ppermute(array, "ctx", pairs)


def dec_move(array, dz):
    return lax.ppermute(array, "dec", [(i, (i + dz) % 8) for i in range(8)])


def body(queries, keys, values, dec_queries, dec_keys, dec_values, page_table, ctx_lengths):
    c = lax.axis_index("ctx")
    z = lax.axis_index("dec")
    x, y, core = c // 4, (c // 2) % 2, c % 2
    chip = c // 2
    meta = jnp.stack([chip, core, x, y, z]).astype(jnp.int32)

    k0, v0 = keys[0], values[0]
    first = jnp.concatenate([k0[:, :HD], v0[:, :HD]], axis=0)
    second = jnp.concatenate([k0[:, HD:], v0[:, HD:]], axis=0)
    mine = jnp.where(core == 0, first, second)
    other = jnp.where(core == 0, second, first)
    barrier = lax.optimization_barrier
    q, other = barrier((queries[0], other))
    got = ctx_move(other, flip_core=1)
    q_oth = ctx_move(lax.dynamic_slice_in_dim(q, (1 - core) * 2048, 2048, 1), flip_core=1)
    got, q_oth, meta = barrier((got, q_oth, meta))
    chunk = jnp.concatenate([mine, got], axis=0)
    lens = jnp.tile(ctx_lengths, 4)[:, None]
    f1, b1 = dec_move(chunk, 1), dec_move(chunk, -1)
    rr, ll, yy = ctx_move(chunk, dx=1), ctx_move(chunk, dx=-1), ctx_move(chunk, flip_y=1)
    f1, b1, rr, ll, yy, lens = barrier((f1, b1, rr, ll, yy, lens))
    near = (chunk, rr, ll, yy)
    up, down, rl = pick(meta, page_table, chunk, f1, b1, rr, ll)
    fs, bs = dec_move(up, 3), dec_move(down, -3)
    yrl, xx = ctx_move(rl, flip_y=1), ctx_move(rr, dx=1)
    pa0 = prefill(meta, q, q_oth, near, 0, 8)
    yrl, xx, fs, bs, pa0 = barrier((yrl, xx, fs, bs, pa0))
    part = decode_part(meta, page_table, dec_queries, dec_keys, dec_values, lens, (chunk, f1, b1, fs, bs))
    part, meta = barrier((part, meta))
    got = [ctx_move(part, mirror_x=k) for k in (1, 2, 3)]
    xy = ctx_move(xx, flip_y=1)
    pa1 = prefill(meta, q, q_oth, near, 8, 8)
    got, xy, pa1 = barrier((got, xy, pa1))
    part = merge(meta, (part, *got), 2)
    part, meta = barrier((part, meta))
    got = ctx_move(part, flip_y=1)
    own_out, oth_out = prefill(meta, q, q_oth, (yrl, xx, xy), 0, 16, (pa0, pa1))
    got, own_out, oth_out = barrier((got, own_out, oth_out))
    back = ctx_move(oth_out, flip_core=1)
    part = merge(meta, (part, got), 3, last=True)
    part, back = barrier((part, back))
    got = ctx_move(part, flip_core=1)
    prefill_out = join(meta, [own_out], [back])
    got, prefill_out = barrier((got, prefill_out))
    decode_out = place(meta, part, got)
    return (prefill_out[None], decode_out)


def solution(mesh):
    return jax.shard_map(
        body,
        mesh=mesh,
        in_specs=(
            P("dec", "ctx", "tp"),
            P("dec", "ctx", "tp"),
            P("dec", "ctx", "tp"),
            P(None, "dec", "tp"),
            P(None, "dec", "tp"),
            P(None, "dec", "tp"),
            P(),
            P("dec"),
        ),
        out_specs=(P("dec", "ctx", "tp"), P(None, "dec", "tp")),
        check_vma=False,
    )
```

```python
import functools

import jax
import jax.numpy as jnp
from jax import lax
from jax.experimental import pallas as pl
from jax.experimental.pallas import tpu as pltpu
from jax.sharding import PartitionSpec as P

HD = 128
PAGE = 128
SCALE = HD**-0.5
LOG2E = 1.4426950408889634
CEXP = SCALE * LOG2E
SAFE = 75.0
NEG = -1e30
NT = (((1,), (1,)), ((), ()))
VMEM_LIMIT = 56 * 2**20
SMALL_LIMIT = 16 * 2**20
F32 = jnp.float32
BF16 = jnp.bfloat16


def dot_nt(a, b):
    return lax.dot_general(a, b, NT, preferred_element_type=F32)


def dot_nn(a, b):
    return jnp.dot(a, b, preferred_element_type=F32)


def row_norm_bound(block, fold):
    sq = block.astype(F32)
    sq = sq * sq
    each = sq.shape[0] // fold
    most = sq[:each]
    for i in range(1, fold):
        most = jnp.maximum(most, sq[i * each : (i + 1) * each])
    return jnp.max(jnp.sum(most, axis=1, keepdims=True), axis=0, keepdims=True)


def prefill_kernel(meta, *refs, group, rows, first):
    chip, core, xpos, ypos = meta[0], meta[1], meta[2], meta[3]
    if first:
        q_own, q_oth, own, rr, ll, yy, state, flag, ks, vx, kbest, sem = refs
    else:
        q_own, q_oth, yrl, xx, xy, before_a, flag_a, before_b, flag_b = refs[:9]
        o_own, o_oth, ks, vx, kbest, acc, sem = refs[-7:]
    step = pl.program_id(0)
    half = 256

    def chip_id(dx, dy):
        return lax.rem(xpos + dx + 4, 4) * 2 + lax.rem(ypos + dy, 2)

    if first:
        pieces = [(chip_id(0, 0), own, 0), (chip_id(-1, 0), rr, 0), (chip_id(1, 0), ll, 0), (chip_id(0, 1), yy, 0)]
    else:
        pieces = [(chip_id(-1, 1), yrl, 0), (chip_id(1, 1), yrl, 1024), (chip_id(2, 0), xx, 0), (chip_id(2, 1), xy, 0)]
    needed = [p[0] <= chip for p in pieces]
    slots, count = [], jnp.int32(0)
    for need in needed:
        slots.append(count)
        count = count + need.astype(jnp.int32)

    def copies(index):
        _, buf, start = pieces[index]
        base = slots[index] * 512
        out = []
        for side in range(2):
            off = start + side * 512
            dst = pl.multiple_of(base + side * half, half)
            out.append(
                pltpu.make_async_copy(
                    buf.at[pl.ds(off, half), :], ks.at[pl.ds(dst, half), :], sem.at[index, 2 * side]
                )
            )
            out.append(
                pltpu.make_async_copy(
                    buf.at[pl.ds(off + half, half), :],
                    vx.at[pl.ds(dst, half), pl.ds(0, HD)],
                    sem.at[index, 2 * side + 1],
                )
            )
        return out

    @pl.when(step == 0)
    def _load():
        for index in range(4):

            @pl.when(needed[index])
            def _start(index=index):
                for copy in copies(index):
                    copy.start()

        vx[:, HD:] = jnp.ones((vx.shape[0], HD), BF16)
        for index in range(4):

            @pl.when(needed[index])
            def _wait(index=index):
                for copy in copies(index):
                    copy.wait()

        def norm(block, best):
            return jnp.maximum(best, row_norm_bound(ks[pl.ds(pl.multiple_of(block * 512, 512), 512), :], 8))

        kbest[0:1, 0:1] = lax.fori_loop(0, count, norm, jnp.zeros((1, 1), F32))

    q_refs = (q_own, q_oth)
    qmax = jnp.zeros((1, 1), F32)
    for q_ref in q_refs:
        for g in range(group):
            qmax = jnp.maximum(qmax, row_norm_bound(q_ref[:, g * HD : (g + 1) * HD], 4))
    bound = qmax * kbest[0:1, 0:1] * (SCALE * SCALE * 1.0001)
    safe = bound[0, 0] <= SAFE * SAFE
    if first:
        flag[step] = jnp.where(safe, 0, 1)
    else:
        later = step >= flag_a.shape[0]
        shifted = jnp.where(later, flag_b[lax.rem(step, flag_b.shape[0])], flag_a[lax.rem(step, flag_a.shape[0])]) != 0
        safe = safe & jnp.logical_not(shifted)

    def tiles(pair):
        for i in range(2):
            g = pair * 2 + i
            cols = pl.ds(pl.multiple_of(g * HD, HD), HD)
            for side in range(2):
                for r in range(half // rows):
                    q = q_refs[side][r * rows : (r + 1) * rows, cols]
                    yield g, side, r, slice(side * half + r * rows, side * half + (r + 1) * rows), q

    def over_pairs(work):
        def one_pair(pair, carry):
            for tile in tiles(pair):
                work(*tile)
            return carry

        lax.fori_loop(0, group // 2, one_pair, 0)

    def allowed(side, r):
        q_pos0 = (core if side == 0 else 1 - core) * half + r * rows
        row = lax.broadcasted_iota(jnp.int32, (rows, half), 0) + q_pos0
        col = lax.broadcasted_iota(jnp.int32, (rows, half), 1)
        return jnp.concatenate([col + core * half <= row, col + (1 - core) * half <= row], axis=1)

    def weighted(q, base, size, ok=None):
        p = jnp.exp2(dot_nt(q, ks[pl.ds(base, size), :]) * CEXP)
        if ok is not None:
            masked = jnp.where(ok, p[:, :512], 0.0)
            p = masked if size == 512 else jnp.concatenate([masked, p[:, 512:]], axis=1)
        return dot_nn(p.astype(BF16), vx[pl.ds(base, size), :])

    def write(g, side, at, both):
        cols = pl.ds(pl.multiple_of(g * HD, HD), HD)
        r = slice(at.start - side * half, at.stop - side * half)
        (o_own, o_oth)[side][r, cols] = (both[:, :HD] / both[:, HD:]).astype(BF16)

    full = count == 4

    def started(g, at):
        return jnp.where(later, before_b[g, at, :], before_a[g, at, :])


    @pl.when(safe & full)
    def _straight():
        def work(g, side, r, at, q):
            if first:
                state[g, at, :] = weighted(q, 0, 2048, allowed(side, r))
            else:
                write(g, side, at, started(g, at) + weighted(q, 0, 2048))

        over_pairs(work)

    @pl.when(safe & jnp.logical_not(full))
    def _plain():
        sums = state if first else acc

        def start(g, side, r, at, q):
            if first:
                sums[g, at, :] = weighted(q, 0, 512, allowed(side, r))
            else:
                sums[g, at, :] = started(g, at)

        over_pairs(start)

        def one(index, carry):
            def add(g, side, r, at, q):
                sums[g, at, :] += weighted(q, pl.multiple_of(index * 512, 512), 512)

            over_pairs(add)
            return carry

        lax.fori_loop(1 if first else 0, count, one, 0)
        if not first:
            over_pairs(lambda g, side, r, at, q: write(g, side, at, sums[g, at, :]))

    @pl.when(jnp.logical_not(safe))
    def _online():
        sums = state if first else acc
        lane = lax.broadcasted_iota(jnp.int32, (rows, 2 * HD), 1)
        for side in range(2):

            def tile(number, carry, side=side):
                g, r = number // (half // rows), lax.rem(number, half // rows)
                q = q_refs[side][pl.ds(pl.multiple_of(r * rows, rows), rows), pl.ds(pl.multiple_of(g * HD, HD), HD)]
                at = pl.ds(pl.multiple_of(side * half + r * rows, rows), rows)
                if first:
                    sums[g, at, :] = jnp.zeros((rows, 2 * HD), F32)
                    best0 = jnp.full((rows, 1), NEG, F32)
                else:
                    old = started(g, at)
                    sums[g, at, :] = jnp.where(lane >= HD, old[:, HD : HD + 1], old)
                    best0 = jnp.where(shifted, old[:, 2 * HD - 1 :], 0.0)
                own_ok = allowed(side, r) if first else None

                def one(index, best):
                    base = pl.multiple_of(index * 512, 512)
                    s = dot_nt(q, ks[pl.ds(base, 512), :]) * SCALE
                    if own_ok is not None:
                        s = jnp.where(jnp.logical_or(own_ok, index > 0), s, NEG)
                    new = jnp.maximum(best, jnp.max(s, axis=1, keepdims=True))
                    p = jnp.exp(s - new)
                    if own_ok is not None:
                        p = jnp.where(jnp.logical_or(own_ok, index > 0), p, 0.0)
                    sums[g, at, :] = sums[g, at, :] * jnp.exp(best - new) + dot_nn(
                        p.astype(BF16), vx[pl.ds(base, 512), :]
                    )
                    return new

                best = lax.fori_loop(0, count, one, best0)
                both = sums[g, at, :]
                if first:
                    sums[g, at, :] = jnp.where(lane == 2 * HD - 1, best, both)
                else:
                    (o_own, o_oth)[side][
                        pl.ds(pl.multiple_of(r * rows, rows), rows), pl.ds(pl.multiple_of(g * HD, HD), HD)
                    ] = (both[:, :HD] / both[:, HD:]).astype(BF16)
                return carry

            lax.fori_loop(0, group * (half // rows), tile, 0)


def prefill(meta, queries, q_oth, bufs, head, heads, before=None, group=4, rows=128):
    per = 16 // group
    at = head // group
    first = before is None
    steps = heads // group
    any_spec = pl.BlockSpec(memory_space=pl.ANY)
    smem = pl.BlockSpec(memory_space=pltpu.SMEM)
    state_shape = (group, 512, 2 * HD)
    in_specs = [
        pl.BlockSpec((256, group * HD), lambda i, m: (0, m[1] * per + at + i)),
        pl.BlockSpec((256, group * HD), lambda i, m: (0, at + i)),
    ] + [any_spec] * len(bufs)
    args = [queries, q_oth, *bufs]
    scratch = [pltpu.VMEM((2048, HD), BF16), pltpu.VMEM((2048, 2 * HD), BF16), pltpu.VMEM((8, HD), F32)]
    if first:
        out_specs = [pl.BlockSpec(state_shape, lambda i, m: (i, 0, 0)), smem]
        out_shape = [
            jax.ShapeDtypeStruct((heads,) + state_shape[1:], F32),
            jax.ShapeDtypeStruct((steps,), jnp.int32),
        ]
    else:
        (sums_a, flags_a), (sums_b, flags_b) = before
        split = sums_a.shape[0] // group
        in_specs += [
            pl.BlockSpec(state_shape, lambda i, m: (jnp.minimum(i, split - 1), 0, 0)),
            smem,
            pl.BlockSpec(state_shape, lambda i, m: (jnp.maximum(i - split, 0), 0, 0)),
            smem,
        ]
        args += [sums_a, flags_a, sums_b, flags_b]
        out_specs = [pl.BlockSpec((256, group * HD), lambda i, m: (0, i))] * 2
        out_shape = [jax.ShapeDtypeStruct((256, heads * HD), BF16)] * 2
        scratch.append(pltpu.VMEM(state_shape, F32))
    scratch.append(pltpu.SemaphoreType.DMA((4, 4)))
    return pl.pallas_call(
        functools.partial(prefill_kernel, group=group, rows=rows, first=first),
        grid_spec=pltpu.PrefetchScalarGridSpec(
            num_scalar_prefetch=1,
            grid=(steps,),
            in_specs=in_specs,
            out_specs=out_specs,
            scratch_shapes=scratch,
        ),
        out_shape=out_shape,
        compiler_params=pltpu.CompilerParams(vmem_limit_bytes=VMEM_LIMIT),
        cost_estimate=pl.CostEstimate(
            flops=8 * 512 * heads * 2048 * HD, bytes_accessed=4 * 2**20, transcendentals=0
        ),
        name="prefill_a" if first else "prefill_b",
    )(meta, *args)


def join_kernel(meta, *refs):
    parts, out, sem = refs[:-2], refs[-2], refs[-1]
    copies = []
    for side in range(2):
        at = (meta[1] if side == 0 else 1 - meta[1]) * 16 * HD
        for part in parts[side * len(parts) // 2 : (side + 1) * len(parts) // 2]:
            wide = part.shape[1]
            copies.append(
                pltpu.make_async_copy(part, out.at[:, pl.ds(pl.multiple_of(at, HD), wide)], sem.at[len(copies)])
            )
            at = at + wide
    for copy in copies:
        copy.start()
    for copy in copies:
        copy.wait()


def join(meta, own, oth):
    parts = [*own, *oth]
    return pl.pallas_call(
        join_kernel,
        grid_spec=pltpu.PrefetchScalarGridSpec(
            num_scalar_prefetch=1,
            grid=(1,),
            in_specs=[pl.BlockSpec(part.shape, lambda i, m: (0, 0)) for part in parts],
            out_specs=pl.BlockSpec(memory_space=pl.ANY),
            scratch_shapes=[pltpu.SemaphoreType.DMA((len(parts),))],
        ),
        out_shape=jax.ShapeDtypeStruct((256, 32 * HD), BF16),
        compiler_params=pltpu.CompilerParams(vmem_limit_bytes=SMALL_LIMIT),
        name="join",
    )(meta, *parts)


def pick_kernel(meta, table, own, f1, b1, rr, ll, up, down, both):
    both[:1024, :] = rr[...]
    both[1024:, :] = ll[...]
    chip, core, z = meta[0], meta[1], meta[4]
    for out, shift in ((up, 3), (down, 5)):
        goal = lax.rem(z + shift, 8)
        for page in range(4):
            side, inner = page // 2, page % 2
            from_core = core if side == 0 else 1 - core
            rel = lax.rem(table[goal, chip * 4 + from_core * 2 + inner] - z + 8, 8)
            for kind in range(2):
                off = side * 512 + kind * 256 + inner * PAGE
                at = slice(off, off + PAGE)
                out[at, :] = jnp.where(rel == 1, b1[at, :], jnp.where(rel == 7, f1[at, :], own[at, :]))


def pick(meta, table, own, f1, b1, rr, ll):
    smem = pl.BlockSpec(memory_space=pltpu.SMEM)
    vmem = pl.BlockSpec(memory_space=pltpu.VMEM)
    return pl.pallas_call(
        pick_kernel,
        in_specs=[smem, smem] + [vmem] * 5,
        out_specs=[vmem] * 3,
        out_shape=[jax.ShapeDtypeStruct((n, HD), BF16) for n in (1024, 1024, 2048)],
        compiler_params=pltpu.CompilerParams(vmem_limit_bytes=SMALL_LIMIT),
        name="pick",
    )(meta, table, own, f1, b1, rr, ll)


def decode_kernel(
    meta, table, q_ref, nk_ref, nv_ref, len_ref, own, f1, b1, fs, bs,
    out, ks, vx, sem,
):
    chip, core, zpos = meta[0], meta[1], meta[4]
    sources = {0: own, 7: f1, 1: b1, 2: bs, 3: bs, 4: fs, 5: fs, 6: fs}

    def page_copy(buf, off, page):
        return (
            pltpu.make_async_copy(
                buf.at[pl.ds(off, PAGE), :], ks.at[pl.ds(page * PAGE, PAGE), :], sem.at[page, 0]
            ),
            pltpu.make_async_copy(
                buf.at[pl.ds(off + 256, PAGE), :],
                vx.at[pl.ds(page * PAGE, PAGE), pl.ds(0, HD)],
                sem.at[page, 1],
            ),
        )

    for page in range(4):
        side, inner = page // 2, page % 2
        from_core = core if side == 0 else 1 - core
        prompt = table[zpos, chip * 4 + from_core * 2 + inner]
        rel = lax.rem(prompt - zpos + 8, 8)
        for r in range(8):
            buf, off = sources[r], side * 512 + inner * PAGE

            @pl.when(rel == r)
            def _start(buf=buf, off=off, page=page):
                for copy in page_copy(buf, off, page):
                    copy.start()

    vx[:, HD:] = jnp.ones((512 + 64, HD), BF16)
    ks[512:, :] = nk_ref[...].reshape(64, HD)
    vx[512:, :HD] = nv_ref[...].reshape(64, HD)
    for page in range(4):
        for copy in page_copy(own, 0, page):
            copy.wait()

    lens = len_ref[...]
    row = lax.broadcasted_iota(jnp.int32, (64, 64), 0)
    col = lax.broadcasted_iota(jnp.int32, (64, 64), 1)
    new_ok = (lax.rem(row, 16) == lax.rem(col, 16)) & (col <= row) & (chip == 0)
    pos = lax.broadcasted_iota(jnp.int32, (64, 256), 1)
    base = chip * 512
    ok0 = pos + (base + core * 256) < lens
    ok1 = pos + (base + (1 - core) * 256) < lens
    ok = jnp.concatenate([ok0, ok1, new_ok], axis=1)
    keys = ks[...]
    vals = vx[...]
    lane = lax.broadcasted_iota(jnp.int32, (64, HD), 1)
    stats = jnp.zeros((64, HD), F32)
    for g0 in range(0, 16, 4):
        qs = [q_ref[:, :, h * HD : (h + 1) * HD].reshape(64, HD) for h in range(g0, g0 + 4)]
        s = dot_nt(jnp.concatenate(qs, axis=0), keys) * SCALE
        s = jnp.where(jnp.concatenate([ok] * 4, axis=0), s, NEG)
        best = jnp.max(s, axis=1, keepdims=True).astype(BF16).astype(F32)
        p = jnp.exp(s - jnp.maximum(best, 0.5 * NEG)).astype(BF16)
        o = dot_nn(p, vals)
        for i in range(4):
            h = g0 + i
            at = slice(i * 64, (i + 1) * 64)
            out[:, h * HD : (h + 1) * HD] = o[at, :HD].astype(BF16)
            total = o[at, HD:]
            high = total.astype(BF16).astype(F32)
            stats = jnp.where(lane == h, best[at], stats)
            stats = jnp.where(lane == 16 + h, high, stats)
            stats = jnp.where(lane == 32 + h, total - high, stats)
    out[:, 16 * HD :] = stats.astype(BF16)


def decode_part(meta, table, dec_q, dec_k, dec_v, lens, bufs):
    any_spec = pl.BlockSpec(memory_space=pl.ANY)
    return pl.pallas_call(
        decode_kernel,
        grid_spec=pltpu.PrefetchScalarGridSpec(
            num_scalar_prefetch=2,
            grid=(1,),
            in_specs=[
                pl.BlockSpec((4, 16, 16 * HD), lambda i, m, t: (0, 0, m[1])),
                pl.BlockSpec((4, 16, HD), lambda i, m, t: (0, 0, m[1])),
                pl.BlockSpec((4, 16, HD), lambda i, m, t: (0, 0, m[1])),
                pl.BlockSpec((64, 1), lambda i, m, t: (0, 0)),
            ]
            + [any_spec] * 5,
            out_specs=pl.BlockSpec((64, 17 * HD), lambda i, m, t: (0, 0)),
            scratch_shapes=[
                pltpu.VMEM((512 + 64, HD), BF16),
                pltpu.VMEM((512 + 64, 2 * HD), BF16),
                pltpu.SemaphoreType.DMA((4, 2)),
            ],
        ),
        out_shape=jax.ShapeDtypeStruct((64, 17 * HD), BF16),
        compiler_params=pltpu.CompilerParams(vmem_limit_bytes=SMALL_LIMIT),
        cost_estimate=pl.CostEstimate(flops=2 * 10**9, bytes_accessed=2**20, transcendentals=0),
        name="decode_part",
    )(meta, table, dec_q, dec_k, dec_v, lens, *bufs)


def merge_kernel(meta, *refs, axis, count, heads, last):
    ins, out, held = refs[:count], refs[count], refs[count + 1]
    for b in range(count):
        held[meta[axis] ^ b] = ins[b][...]
    ins = [held.at[k] for k in range(count)]
    cols = heads * HD
    lane = lax.broadcasted_iota(jnp.int32, (64, HD), 1)
    stats_in = [ref[:, cols:].astype(F32) for ref in ins]

    def total_of(stat):
        return pltpu.roll(stat, HD - 16, 1) + pltpu.roll(stat, HD - 32, 1)

    best = functools.reduce(jnp.maximum, stats_in)
    shares = [jnp.exp(stat - best) for stat in stats_in]
    total = sum(total_of(stat) * w for stat, w in zip(stats_in, shares))
    used = lane < heads
    if last:
        inverse = 1.0 / jnp.where(used, total, 1.0)
        shares = [w * inverse for w in shares]
    place = lax.broadcasted_iota(jnp.int32, (HD, cols), 0) == (
        lax.broadcasted_iota(jnp.int32, (HD, cols), 1) // HD
    )
    place = place.astype(BF16)

    def spread(w):
        w = jnp.where(used, w, 0.0)
        high = w.astype(BF16)
        low = (w - high.astype(F32)).astype(BF16)
        return dot_nn(high, place) + dot_nn(low, place)

    joined = sum(ref[:, :cols].astype(F32) * spread(w) for ref, w in zip(ins, shares))
    out[:, :cols] = joined.astype(BF16)
    if last:
        return
    high = total.astype(BF16).astype(F32)
    stats = jnp.zeros((64, HD), F32)
    for values, goal in ((best, 0), (high, 16), (total - high, 32)):
        moved = pltpu.roll(values, goal, 1) if goal else values
        stats = jnp.where((lane >= goal) & (lane < goal + heads), moved, stats)
    out[:, cols:] = stats.astype(BF16)


def merge(meta, parts, axis, heads=16, last=False):
    width = heads * HD if last else (heads + 1) * HD
    vmem = pl.BlockSpec(memory_space=pltpu.VMEM)
    return pl.pallas_call(
        functools.partial(merge_kernel, axis=axis, count=len(parts), heads=heads, last=last),
        in_specs=[pl.BlockSpec(memory_space=pltpu.SMEM)] + [vmem] * len(parts),
        out_specs=vmem,
        scratch_shapes=[pltpu.VMEM((len(parts), 64, (heads + 1) * HD), BF16)],
        out_shape=jax.ShapeDtypeStruct((64, width), BF16),
        compiler_params=pltpu.CompilerParams(vmem_limit_bytes=SMALL_LIMIT),
        cost_estimate=pl.CostEstimate(flops=10**6, bytes_accessed=2**18, transcendentals=0),
        name="merge",
    )(meta, *parts)


def place_kernel(meta, own, oth, out, sem):
    copies = []
    for side, ref in enumerate((own, oth)):
        at = pl.multiple_of((meta[1] if side == 0 else 1 - meta[1]) * 16 * HD, 16 * HD)
        copies.append(pltpu.make_async_copy(ref, out.at[:, :, pl.ds(at, 16 * HD)], sem.at[side]))
    for copy in copies:
        copy.start()
    for copy in copies:
        copy.wait()


def place(meta, own, oth):
    return pl.pallas_call(
        place_kernel,
        in_specs=[pl.BlockSpec(memory_space=pltpu.SMEM)] + [pl.BlockSpec(memory_space=pltpu.VMEM)] * 2,
        out_specs=pl.BlockSpec(memory_space=pl.ANY),
        scratch_shapes=[pltpu.SemaphoreType.DMA((2,))],
        out_shape=jax.ShapeDtypeStruct((4, 16, 4096), BF16),
        name="place",
    )(meta, own.reshape(4, 16, 2048), oth.reshape(4, 16, 2048))


def ctx_move(array, dx=0, flip_y=0, flip_core=0, mirror_x=0):
    pairs = []
    for c in range(16):
        x, y, core = c // 4, (c // 2) % 2, c % 2
        to_x = ((x + dx) % 4) ^ mirror_x
        pairs.append((c, to_x * 4 + (y ^ flip_y) * 2 + (core ^ flip_core)))
    return lax.ppermute(array, "ctx", pairs)


def dec_move(array, dz):
    return lax.ppermute(array, "dec", [(i, (i + dz) % 8) for i in range(8)])


def body(queries, keys, values, dec_queries, dec_keys, dec_values, page_table, ctx_lengths):
    c = lax.axis_index("ctx")
    z = lax.axis_index("dec")
    x, y, core = c // 4, (c // 2) % 2, c % 2
    chip = c // 2
    meta = jnp.stack([chip, core, x, y, z]).astype(jnp.int32)

    k0, v0 = keys[0], values[0]
    first = jnp.concatenate([k0[:, :HD], v0[:, :HD]], axis=0)
    second = jnp.concatenate([k0[:, HD:], v0[:, HD:]], axis=0)
    mine = jnp.where(core == 0, first, second)
    other = jnp.where(core == 0, second, first)
    barrier = lax.optimization_barrier
    q, other = barrier((queries[0], other))
    got = ctx_move(other, flip_core=1)
    q_oth = ctx_move(lax.dynamic_slice_in_dim(q, (1 - core) * 2048, 2048, 1), flip_core=1)
    got, q_oth, meta = barrier((got, q_oth, meta))
    chunk = jnp.concatenate([mine, got], axis=0)
    lens = jnp.tile(ctx_lengths, 4)[:, None]
    f1, b1 = dec_move(chunk, 1), dec_move(chunk, -1)
    rr, ll, yy = ctx_move(chunk, dx=1), ctx_move(chunk, dx=-1), ctx_move(chunk, flip_y=1)
    f1, b1, rr, ll, yy, lens = barrier((f1, b1, rr, ll, yy, lens))
    near = (chunk, rr, ll, yy)
    up, down, rl = pick(meta, page_table, chunk, f1, b1, rr, ll)
    fs, bs = dec_move(up, 3), dec_move(down, -3)
    yrl, xx = ctx_move(rl, flip_y=1), ctx_move(rr, dx=1)
    pa0 = prefill(meta, q, q_oth, near, 0, 8)
    yrl, xx, fs, bs, pa0 = barrier((yrl, xx, fs, bs, pa0))
    part = decode_part(meta, page_table, dec_queries, dec_keys, dec_values, lens, (chunk, f1, b1, fs, bs))
    part, meta = barrier((part, meta))
    got = [ctx_move(part, mirror_x=k) for k in (1, 2, 3)]
    xy = ctx_move(xx, flip_y=1)
    pa1 = prefill(meta, q, q_oth, near, 8, 8)
    got, xy, pa1 = barrier((got, xy, pa1))
    part = merge(meta, (part, *got), 2)
    part, meta = barrier((part, meta))
    got = ctx_move(part, flip_y=1)
    own_out, oth_out = prefill(meta, q, q_oth, (yrl, xx, xy), 0, 16, (pa0, pa1))
    got, own_out, oth_out = barrier((got, own_out, oth_out))
    back = ctx_move(oth_out, flip_core=1)
    part = merge(meta, (part, got), 3, last=True)
    part, back = barrier((part, back))
    got = ctx_move(part, flip_core=1)
    prefill_out = join(meta, [own_out], [back])
    got, prefill_out = barrier((got, prefill_out))
    decode_out = place(meta, part, got)
    return (prefill_out[None], decode_out)


def solution(mesh):
    return jax.shard_map(
        body,
        mesh=mesh,
        in_specs=(
            P("dec", "ctx", "tp"),
            P("dec", "ctx", "tp"),
            P("dec", "ctx", "tp"),
            P(None, "dec", "tp"),
            P(None, "dec", "tp"),
            P(None, "dec", "tp"),
            P(),
            P("dec"),
        ),
        out_specs=(P("dec", "ctx", "tp"), P(None, "dec", "tp")),
        check_vma=False,
    )
```
